256 devices in a mesh: prow: 8 (over x, core), pcol: 32 (over z, y).
Axes of the slice: x: 4, y: 4, z: 8, core: 2. Of those that a mesh axis runs over, the one named last changes fastest.
Arguments:
- rhs: float32 [64, 65536], P(None, 'pcol'), may hold values from -6 to 6
- pivots: int32 [65536], P('pcol'), may hold values from 0 to 65535, as said below
- tile_of: int32 [256], replicated, may hold values from 0 to 255, as said below
- upper_rows: bfloat16 [3, 2048, 65536], P(None, 'prow', 'pcol'), may hold values from -0.125 to 0.125
- upper_inv: bfloat16 [3, 2048, 2048], P(None, 'pcol', 'prow'), may hold values from -0.125 to 0.125
- lower_rows: bfloat16 [3, 2048, 65536], P(None, 'prow', 'pcol'), may hold values from -0.125 to 0.125
- lower_inv: bfloat16 [3, 2048, 2048], P(None, 'prow', 'pcol'), may hold values from -0.125 to 0.125
- solved: float32 [64, 65536], P(None, 'pcol'), may hold values from -6 to 6
Outputs:
- forward: float32 [64, 65536], P(None, 'pcol')
- backward: float32 [64, 65536], P(None, 'pcol')
The draws below stay inside these ranges and needn't reach their ends.
Inputs may be any that keep to these rules, and one draw needn't show every extreme that they name: pivots[p] lies in the same tile of 256 storage columns as p, and each column of a tile appears once. `tile_of`: storage tile d * 256 / 32 + l holds global tile l * 32 + c(d), c a permutation of the process columns.
All inputs are finite; a program needn't handle non-finite values.
Results may differ from the reference program's by a relative error of at most 0.015.
Values may be sent and summed in bfloat16 or wider, within the bound.
No kernel may reach another device: no remote copies, remote signals or barrier semaphores. Data moves between devices by JAX's collectives and lax.ppermute only.
A program may use at most 64 MiB of HBM per device.

```python
import jax
import jax.numpy as jnp

N = 65536
NB = 2048
TILE = 256
R = 64
STEPS = 3
NT = 256
N_PCOL = 32


def draw_pivots(key, part):
    key = jax.random.fold_in(key, 17)
    keys = jax.random.split(key, NT)
    orders = jax.vmap(lambda single: jax.random.permutation(single, TILE))(keys)
    starts = jnp.arange(NT, dtype=jnp.int32)[:, None] * TILE
    return (starts + orders.astype(jnp.int32)).reshape(N).astype(jnp.int32)


def draw_tile_of(key, part):
    key = jax.random.fold_in(key, 11)
    columns = jax.random.permutation(key, N_PCOL).astype(jnp.int32)
    tiles_here = NT // N_PCOL
    slots = jnp.arange(NT, dtype=jnp.int32)
    return (slots % tiles_here * N_PCOL + columns[slots // tiles_here]).astype(jnp.int32)


def levels(rng, dims, cuts, low, top_value):
    def one(axis_at, shards_of):
        draws = jax.random.uniform(jax.random.fold_in(jax.random.fold_in(rng, 6), axis_at), (shards_of,), jnp.float32, low / len(cuts), top_value / len(cuts))
        return jnp.repeat(jnp.exp(draws), dims[axis_at] // shards_of).reshape((-1,) + (1,) * (len(dims) - axis_at - 1))

    gain = one(*cuts[0])
    for cut in cuts[1:]:
        gain = gain * one(*cut)
    return gain


def noise(key, extent, scale, limit, cuts=(), held_as=jnp.bfloat16):
    loudness = levels(key, extent, cuts, -0.22, 0.18) if cuts else 1.0
    array = jax.random.normal(key, extent, jnp.float32) * scale * loudness
    return jnp.minimum(jnp.maximum(array, -limit), limit).astype(held_as)


def setup_inputs(seed: int = 0) -> dict:
    arg_keys = jax.random.split(jax.random.key(seed), 9)
    rhs = noise(arg_keys[0], (R, N), 1.0, 6.0, ((1, 32),), jnp.float32)
    pivots = draw_pivots(jax.random.fold_in(arg_keys[8], 71), 0)
    tile_of = draw_tile_of(jax.random.fold_in(arg_keys[8], 71), 0)
    upper_rows = noise(arg_keys[3], (STEPS, NB, N), NB ** -0.5, 0.125, ((1, 8), (2, 32)))
    upper_inv = noise(arg_keys[4], (STEPS, NB, NB), NB ** -0.5, 0.125, ((1, 32), (2, 8)))
    lower_rows = noise(arg_keys[5], (STEPS, NB, N), NB ** -0.5, 0.125, ((1, 8), (2, 32)))
    lower_inv = noise(arg_keys[6], (STEPS, NB, NB), NB ** -0.5, 0.125, ((1, 8), (2, 32)))
    solved = noise(arg_keys[7], (R, N), 1.0, 6.0, ((1, 32),), jnp.float32)
    return {"rhs": rhs, "pivots": pivots, "tile_of": tile_of, "upper_rows": upper_rows, "upper_inv": upper_inv, "lower_rows": lower_rows, "lower_inv": lower_inv, "solved": solved}


def reference(rhs, pivots, tile_of, upper_rows, upper_inv, lower_rows, lower_inv, solved):
    cells = jnp.arange(N)
    tiles_block = NB // TILE
    global_tile = tile_of[cells // TILE]
    block_of = global_tile // tiles_block
    place = (global_tile % tiles_block) * TILE + cells % TILE
    state = rhs[:, pivots]
    finished = []
    for step in range(STEPS):
        target = jnp.where(block_of == step, place, NB)
        gathered = jnp.zeros((R, NB + 1), state.dtype).at[:, target].add(state)[:, :NB]
        solved_block = jnp.dot(gathered.astype(jnp.bfloat16), upper_inv[step], preferred_element_type=jnp.float32).astype(jnp.bfloat16)
        update = jnp.dot(solved_block, upper_rows[step], preferred_element_type=jnp.float32)
        state = state - jnp.where(block_of > step, update, 0.0)
        state = jnp.where(block_of == step, solved_block[:, place].astype(jnp.float32), state)
        finished.append(solved_block)
    solution = solved
    for step in reversed(range(STEPS)):
        known = jnp.where(block_of > step, solution, 0.0).astype(jnp.bfloat16)
        sums = jnp.dot(known, lower_rows[step].T, preferred_element_type=jnp.float32)
        resid = (finished[step].astype(jnp.float32) - sums).astype(jnp.bfloat16)
        new_block = jnp.dot(resid, lower_inv[step], preferred_element_type=jnp.float32).astype(jnp.bfloat16)
        solution = jnp.where(block_of == step, new_block[:, place].astype(jnp.float32), solution)
    return state, solution
```

```python
import jax
import jax.numpy as jnp
from jax import lax
from jax.sharding import PartitionSpec as P

NB = 2048
TILE = 256
STEPS = 3
NY = 4
NZ = 8
NP = 8
NC = 32
PER = NB // TILE
Y_GROUPS = [[z * NY + y for y in range(NY)] for z in range(NZ)]
Z_GROUPS = [[z * NY + y for z in range(NZ)] for y in range(NY)]
BF = jnp.bfloat16
F32 = jnp.float32


def swap_y(x):
    return lax.all_to_all(x, "pcol", 0, 0, axis_index_groups=Y_GROUPS, tiled=True)


def swap_z(x):
    return lax.all_to_all(x, "pcol", 0, 0, axis_index_groups=Z_GROUPS, tiled=True)


def swap_pcol(x):
    return lax.all_to_all(x, "pcol", 0, 0, tiled=True)


def swap_prow(x):
    return lax.all_to_all(x, "prow", 0, 0, tiled=True)


def to_all(x, count):
    return jnp.broadcast_to(x[None], (count,) + x.shape)


def total(x):
    return jnp.sum(x.astype(F32), axis=0)


def choose(values, index):
    where = (index[:, None] == jnp.arange(values.shape[0])[None, :]).astype(BF)
    flat = jnp.dot(where, values.reshape(values.shape[0], -1), preferred_element_type=F32)
    return flat.astype(BF).reshape((index.shape[0],) + values.shape[1:])


def body(rhs, pivots, tile_of, upper_rows, upper_inv, lower_rows, lower_inv, solved):
    col = lax.axis_index("pcol")
    row = lax.axis_index("prow")
    z = col // NY
    count, width = rhs.shape
    slots = width // TILE
    rows_z = count // NY
    rows_own = count // NC
    first_tiles = tile_of.reshape(NC, slots)[:, 0]
    my_tile = first_tiles[col]
    my_block = my_tile // PER
    my_place = my_tile % PER
    plane_tiles = lax.dynamic_slice_in_dim(first_tiles, z * NY, NY)
    plane_blocks = plane_tiles // PER

    lower_pack = jnp.concatenate(
        [
            jnp.swapaxes(lower_inv, 1, 2).reshape(STEPS * (NB // NC), TILE),
            lower_rows[: STEPS - 1, :, :TILE].reshape((STEPS - 1) * TILE, TILE),
        ],
        axis=0,
    )
    lower_all = lax.all_gather(lower_pack, "pcol", axis=0)

    local_pivots = pivots - col * width
    own = jnp.take(rhs[:, :TILE], local_pivots[:TILE], axis=1)
    state0 = jnp.take(rhs, local_pivots, axis=1)

    own = own.reshape(NZ, NY, rows_own, TILE).transpose(1, 0, 2, 3).reshape(NY, rows_z, TILE)
    own_high = own.astype(BF)
    own_low = (own - own_high.astype(F32)).astype(BF)
    upper_pack = jnp.concatenate(
        [
            upper_inv.reshape(STEPS * (NB // NC), TILE),
            upper_rows[: STEPS - 1, :, :TILE].reshape((STEPS - 1) * TILE, TILE),
        ],
        axis=0,
    )
    got = swap_y(jnp.concatenate([own_high, own_low, to_all(upper_pack, NY)], axis=1))
    tiles = got[:, :rows_z].astype(F32) + got[:, rows_z : 2 * rows_z].astype(F32)
    at = 2 * rows_z
    inverse = []
    for step in range(STEPS):
        inverse.append(got[:, at : at + NB // NC].reshape(TILE, TILE))
        at += NB // NC
    upper_tiles = []
    for step in range(STEPS - 1):
        upper_tiles.append(got[:, at : at + TILE])
        at += TILE

    slot_known = jnp.where(my_block >= STEPS, solved[:, :TILE], 0.0)
    known = jnp.concatenate([slot_known, solved[:, TILE:]], axis=1).astype(BF)
    outer = lax.dot_general(
        known, lower_rows, (((1,), (2,)), ((), ())), preferred_element_type=F32
    )
    outer = outer.astype(BF).reshape(NZ, NY * rows_own * STEPS, TILE)

    finished = []
    for step in range(STEPS):
        block = tiles.astype(BF)
        pick = plane_tiles[None, :] == step * PER + jnp.arange(NZ)[:, None]
        routed = jnp.sum(jnp.where(pick[:, :, None, None], block[None], 0), axis=1)
        mine = jnp.sum(swap_z(routed), axis=0)
        part = jnp.dot(mine, inverse[step], preferred_element_type=F32).astype(BF)
        message = to_all(part, NZ)
        if step == 1:
            message = jnp.concatenate([message, outer], axis=1)
        back = total(swap_z(message))
        solved_rows = back[:rows_z].astype(BF)
        if step == 1:
            outer_sum = back[rows_z:]
        finished.append(solved_rows)
        if step < STEPS - 1:
            update = lax.dot_general(
                solved_rows,
                upper_tiles[step],
                (((1,), (1,)), ((), ())),
                preferred_element_type=F32,
            )
            update = total(swap_prow(to_all(update.astype(BF), NP)))
            update = update.transpose(1, 0, 2)
            tiles = tiles - jnp.where((plane_blocks > step)[:, None, None], update, 0.0)

    stacked = jnp.concatenate(finished, axis=0)
    outer_send = outer_sum.astype(BF).reshape(NY, rows_own * STEPS, TILE)
    got = swap_y(jnp.concatenate([outer_send, to_all(stacked, NY)], axis=1))
    outer_rows = total(got[:, : rows_own * STEPS]).reshape(rows_own, STEPS, TILE)
    every = got[:, rows_own * STEPS :].reshape(NY, STEPS, NZ, rows_own, TILE)
    every = every.transpose(1, 2, 0, 3, 4).reshape(STEPS, count, TILE)

    bulk = jnp.dot(
        jnp.concatenate(list(every), axis=1),
        upper_rows.reshape(STEPS * TILE, width),
        preferred_element_type=F32,
    )
    window_value = jnp.where(
        my_place == row, lax.dynamic_index_in_dim(every, jnp.minimum(my_block, STEPS - 1), 0, False), 0
    ).astype(F32)
    slot_bulk = jnp.where(my_block < STEPS, window_value, bulk[:, :TILE])
    bulk = jnp.concatenate([slot_bulk, bulk[:, TILE:]], axis=1).astype(BF)
    bulk = bulk.reshape(NP, count // NP, width)

    inverse_rows = STEPS * (NB // NC)
    found = [None] * STEPS
    later = [outer_rows[:, step] for step in range(STEPS)]
    for step in reversed(range(STEPS)):
        own_rows = lax.dynamic_slice_in_dim(finished[step], z * rows_own, rows_own, 0)
        resid = (own_rows.astype(F32) - later[step]).astype(BF)
        weights = lower_all[:, step * (NB // NC) : (step + 1) * (NB // NC)].reshape(NB, TILE)
        part = lax.dot_general(
            resid, weights, (((1,), (1,)), ((), ())), preferred_element_type=F32
        ).astype(BF)
        message = to_all(part, NP)
        if step == 1:
            message = jnp.concatenate([message, bulk], axis=1)
        if step == 0:
            message = jnp.concatenate([message, to_all(bulk_sum, NP)], axis=1)
        back = swap_prow(message)
        if step == 1:
            bulk_sum = total(back[:, rows_own:]).astype(BF)
        if step == 0:
            bulk_all = back[:, rows_own:].reshape(count, width).astype(F32)
        value = total(back[:, :rows_own]).astype(BF)
        value = value.reshape(rows_own, PER, TILE).transpose(1, 0, 2)
        found[step] = value
        for earlier in range(step):
            spread = choose(value, first_tiles - step * PER)
            start = inverse_rows + earlier * TILE
            piece = lax.dot_general(
                spread,
                lower_all[:, start : start + TILE],
                (((2,), (2,)), ((0,), (0,))),
                preferred_element_type=F32,
            )
            later[earlier] = later[earlier] + jnp.sum(piece, axis=0)

    window = jnp.concatenate(found, axis=0)
    window = swap_pcol(choose(window, first_tiles)).reshape(count, TILE).astype(F32)
    slot_solution = jnp.where(my_block < STEPS, window, solved[:, :TILE])
    backward = jnp.concatenate([slot_solution, solved[:, TILE:]], axis=1)
    slot_forward = jnp.where(
        my_block < STEPS, bulk_all[:, :TILE], state0[:, :TILE] - bulk_all[:, :TILE]
    )
    forward = jnp.concatenate([slot_forward, state0[:, TILE:] - bulk_all[:, TILE:]], axis=1)
    return (forward, backward)


def solution(mesh):
    return jax.shard_map(
        body,
        mesh=mesh,
        in_specs=(
            P(None, "pcol"),
            P("pcol"),
            P(),
            P(None, "prow", "pcol"),
            P(None, "pcol", "prow"),
            P(None, "prow", "pcol"),
            P(None, "prow", "pcol"),
            P(None, "pcol"),
        ),
        out_specs=(P(None, "pcol"), P(None, "pcol")),
        check_vma=False,
    )
```

```python
import jax
import jax.numpy as jnp
from jax import lax
from jax.experimental import pallas as pl
from jax.experimental.pallas import tpu as pltpu
from jax.sharding import PartitionSpec as P

NB = 2048
TILE = 256
STEPS = 3
NY = 4
NZ = 8
NP = 8
NC = 32
PER = NB // TILE
PIECE = NB // NC
Y_GROUPS = [[z * NY + y for y in range(NY)] for z in range(NZ)]
Z_GROUPS = [[z * NY + y for z in range(NZ)] for y in range(NY)]
BF = jnp.bfloat16
F32 = jnp.float32
UPPER_AT = STEPS * PIECE
LOWER_AT = UPPER_AT + PIECE
PACK = LOWER_AT + (STEPS - 1) * TILE
ROWS = 16


def swap_y(x):
    return lax.all_to_all(x, "pcol", 0, 0, axis_index_groups=Y_GROUPS, tiled=True)


def swap_z(x):
    return lax.all_to_all(x, "pcol", 0, 0, axis_index_groups=Z_GROUPS, tiled=True)


def swap_pcol(x):
    return lax.all_to_all(x, "pcol", 0, 0, tiled=True)


def swap_prow(x):
    return lax.all_to_all(x, "prow", 0, 0, tiled=True)


def to_all(x, count):
    return jnp.broadcast_to(x[None], (count,) + x.shape)


def total(x):
    return jnp.sum(x.astype(F32), axis=0)


def choose(values, index):
    where = (index[:, None] == jnp.arange(values.shape[0])[None, :]).astype(BF)
    flat = jnp.dot(where, values.reshape(values.shape[0], -1), preferred_element_type=F32)
    return flat.astype(BF).reshape((index.shape[0],) + values.shape[1:])


def dot_nt(a, b):
    return lax.dot_general(a, b, (((1,), (1,)), ((), ())), preferred_element_type=F32)


def dot_nn(a, b):
    return jnp.dot(a, b, preferred_element_type=F32)


def place_mask(place):
    return lax.broadcasted_iota(jnp.int32, (ROWS, TILE), 0) % PER == place


def lower_part(resid, inverse):
    part = jnp.zeros((ROWS, TILE), F32)
    for place in range(PER):
        weights = inverse[4 * place : 4 * place + 4].reshape(TILE, TILE)
        part = jnp.where(place_mask(place), dot_nt(resid, weights), part)
    return part.astype(BF)


def last_kernel(pos, got, pick_own, outer, pack, solved_out, message_out, upper, inverse, sems):
    copies = [
        pltpu.make_async_copy(pack.at[:, pl.ds(UPPER_AT, PIECE), :], upper, sems.at[0]),
        pltpu.make_async_copy(
            pack.at[:, pl.ds((STEPS - 1) * PIECE, PIECE), :], inverse, sems.at[1]
        ),
    ]
    for copy in copies:
        copy.start()
    copies[0].wait()
    value = jnp.zeros((ROWS, TILE), F32)
    for place in range(PER):
        weights = upper[4 * place : 4 * place + 4].reshape(TILE, TILE)
        value = value + dot_nn(got[pos[(STEPS - 1) * PER + place]], weights)
    value = value.astype(BF)
    solved_out[...] = value
    resid = (dot_nn(pick_own[...], value) - outer[...]).astype(BF)
    copies[1].wait()
    part = lower_part(resid, inverse)
    for index in range(NP):
        message_out[index] = part


def last_call(pos, got, pick_own, outer, pack):
    vmem = pl.BlockSpec(memory_space=pltpu.VMEM)
    return pl.pallas_call(
        last_kernel,
        out_shape=(
            jax.ShapeDtypeStruct((ROWS, TILE), BF),
            jax.ShapeDtypeStruct((NP, ROWS, TILE), BF),
        ),
        in_specs=[
            pl.BlockSpec(memory_space=pltpu.SMEM),
            vmem,
            vmem,
            vmem,
            pl.BlockSpec(memory_space=pl.ANY),
        ],
        out_specs=(vmem, vmem),
        scratch_shapes=[
            pltpu.VMEM((NC, PIECE, TILE), BF),
            pltpu.VMEM((NC, PIECE, TILE), BF),
            pltpu.SemaphoreType.DMA((2,)),
        ],
        compiler_params=pltpu.CompilerParams(vmem_limit_bytes=24 << 20),
        name="last_block",
    )(pos, got, pick_own, outer, pack)


def lower_kernel(step, pos, back, base, *rest):
    known = rest[: STEPS - 2 - step]
    pack, value_out, message_out, tiles, inverse, sems = rest[STEPS - 2 - step :]
    later = list(range(step + 1, STEPS))
    first = pltpu.make_async_copy(
        pack.at[:, pl.ds(step * PIECE, PIECE), :], inverse, sems.at[len(later) * PER]
    )
    copies = []
    for at, block in enumerate(later):
        for place in range(PER):
            slot = at * PER + place
            copy = pltpu.make_async_copy(
                pack.at[pos[block * PER + place], pl.ds(LOWER_AT + step * TILE, TILE), :],
                tiles.at[slot],
                sems.at[slot],
            )
            copy.start()
            copies.append(copy)
    first.start()
    value = jnp.sum(back[...].astype(F32), axis=0).astype(BF)
    value_out[...] = value
    sums = jnp.zeros((ROWS, TILE), F32)
    for at in reversed(range(len(later))):
        solved = value if at == 0 else known[at - 1][...]
        for place in range(PER):
            slot = at * PER + place
            copies[slot].wait()
            product = dot_nt(solved, tiles[slot])
            sums = sums + jnp.where(place_mask(place), product, 0.0)
    sums = jnp.sum(sums.reshape(ROWS // PER, PER, TILE), axis=1, keepdims=True)
    sums = jnp.broadcast_to(sums, (ROWS // PER, PER, TILE)).reshape(ROWS, TILE)
    resid = (base[...] - sums).astype(BF)
    first.wait()
    part = lower_part(resid, inverse)
    for index in range(NP):
        message_out[index] = part


def lower_call(step, pos, back, base, known, pack):
    vmem = pl.BlockSpec(memory_space=pltpu.VMEM)
    count = (STEPS - 1 - step) * PER
    return pl.pallas_call(
        lambda *refs: lower_kernel(step, *refs),
        out_shape=(
            jax.ShapeDtypeStruct((ROWS, TILE), BF),
            jax.ShapeDtypeStruct((NP, ROWS, TILE), BF),
        ),
        in_specs=[pl.BlockSpec(memory_space=pltpu.SMEM), vmem, vmem]
        + [vmem] * len(known)
        + [pl.BlockSpec(memory_space=pl.ANY)],
        out_specs=(vmem, vmem),
        scratch_shapes=[
            pltpu.VMEM((count, TILE, TILE), BF),
            pltpu.VMEM((NC, PIECE, TILE), BF),
            pltpu.SemaphoreType.DMA((count + 1,)),
        ],
        compiler_params=pltpu.CompilerParams(vmem_limit_bytes=24 << 20),
        name=f"lower_block_{step}",
    )(pos, back, base, *known, pack)


def body(rhs, pivots, tile_of, upper_rows, upper_inv, lower_rows, lower_inv, solved):
    col = lax.axis_index("pcol")
    row = lax.axis_index("prow")
    z = col // NY
    count, width = rhs.shape
    slots = width // TILE
    rows_z = count // NY
    rows_own = count // NC
    first_tiles = tile_of.reshape(NC, slots)[:, 0]
    my_tile = first_tiles[col]
    my_block = my_tile // PER
    my_place = my_tile % PER
    plane_tiles = lax.dynamic_slice_in_dim(first_tiles, z * NY, NY)
    plane_blocks = plane_tiles // PER
    pos = jnp.sum(
        jnp.where(
            first_tiles[None, :] == jnp.arange(STEPS * PER)[:, None],
            jnp.arange(NC, dtype=jnp.int32)[None, :],
            0,
        ),
        axis=1,
        dtype=jnp.int32,
    )

    pack = jnp.concatenate(
        [
            jnp.swapaxes(lower_inv, 1, 2).reshape(STEPS * PIECE, TILE),
            upper_inv[STEPS - 1],
            lower_rows[: STEPS - 1, :, :TILE].reshape((STEPS - 1) * TILE, TILE),
        ],
        axis=0,
    )
    pack_all = lax.all_gather(pack, "pcol", axis=0)

    local_pivots = pivots - col * width
    own = jnp.take(rhs[:, :TILE], local_pivots[:TILE], axis=1)
    own = own.reshape(NZ, NY, rows_own, TILE).transpose(1, 0, 2, 3).reshape(NY, rows_z, TILE)
    own_high = own.astype(BF)
    own_low = (own - own_high.astype(F32)).astype(BF)
    got = swap_y(jnp.concatenate([own_high, own_low, to_all(upper_inv[0], NY)], axis=1))
    tiles = got[:, :rows_z].astype(F32) + got[:, rows_z : 2 * rows_z].astype(F32)
    inverse = [got[:, 2 * rows_z :].reshape(TILE, TILE)]

    slot_known = jnp.where(my_block >= STEPS, solved[:, :TILE], 0.0)
    known = jnp.concatenate([slot_known, solved[:, TILE:]], axis=1).astype(BF)
    outer = lax.dot_general(
        known, lower_rows, (((1,), (2,)), ((), ())), preferred_element_type=F32
    )
    outer = outer.astype(BF).reshape(NZ, NY, rows_own, STEPS, TILE).transpose(1, 0, 2, 3, 4)
    outer = outer.reshape(NY, NZ * rows_own * STEPS, TILE)
    upper_pack = jnp.concatenate(
        [upper_rows[: STEPS - 1, :, :TILE].reshape((STEPS - 1) * TILE, TILE), upper_inv[1]], axis=0
    )
    got = swap_y(jnp.concatenate([to_all(upper_pack, NY), outer], axis=1))
    upper_tiles = [got[:, step * TILE : (step + 1) * TILE] for step in range(STEPS - 1)]
    at = (STEPS - 1) * TILE
    inverse.append(got[:, at : at + PIECE].reshape(TILE, TILE))
    outer = total(got[:, at + PIECE :]).astype(BF).reshape(NZ, rows_own * STEPS, TILE)

    finished = []
    for step in range(STEPS - 1):
        block = tiles.astype(BF)
        pick = plane_tiles[None, :] == step * PER + jnp.arange(NZ)[:, None]
        routed = jnp.sum(jnp.where(pick[:, :, None, None], block[None], 0), axis=1)
        mine = jnp.sum(swap_z(routed), axis=0)
        part = jnp.dot(mine, inverse[step], preferred_element_type=F32).astype(BF)
        message = to_all(part, NZ)
        if step == 1:
            message = jnp.concatenate([message, outer], axis=1)
        back = total(swap_z(message))
        solved_rows = back[:rows_z].astype(BF)
        if step == 1:
            outer = back[rows_z:].reshape(rows_own, STEPS, TILE)
        finished.append(solved_rows)
        update = lax.dot_general(
            solved_rows, upper_tiles[step], (((1,), (1,)), ((), ())), preferred_element_type=F32
        )
        update = total(swap_prow(to_all(update.astype(BF), NP)))
        update = update.transpose(1, 0, 2)
        tiles = tiles - jnp.where((plane_blocks > step)[:, None, None], update, 0.0)

    got = swap_z(to_all(tiles.astype(BF), NZ).reshape(NZ * NY, rows_z, TILE))
    order = jnp.arange(ROWS)
    pick_own = (
        (order[None, :] // rows_own == z) & (order[None, :] % rows_own == order[:, None] // PER)
    ).astype(BF)
    outer = jnp.repeat(outer.transpose(1, 0, 2), PER, axis=1)
    last, message = last_call(pos, got, pick_own, outer[STEPS - 1], pack_all)
    finished.append(last)
    bases = [
        jnp.dot(pick_own, finished[step], preferred_element_type=F32) - outer[step]
        for step in range(STEPS - 1)
    ]

    stacked, message = lax.optimization_barrier((jnp.concatenate(finished, axis=0), message))
    every = swap_y(to_all(stacked, NY)).reshape(NY, STEPS, NZ, rows_own, TILE)
    every = every.transpose(1, 2, 0, 3, 4).reshape(STEPS, count, TILE)
    bulk = jnp.dot(
        jnp.concatenate(list(every), axis=1),
        upper_rows.reshape(STEPS * TILE, width),
        preferred_element_type=F32,
    )
    window_value = jnp.where(
        my_place == row, lax.dynamic_index_in_dim(every, jnp.minimum(my_block, STEPS - 1), 0, False), 0
    ).astype(F32)
    slot_bulk = jnp.where(my_block < STEPS, window_value, bulk[:, :TILE])
    bulk = jnp.concatenate([slot_bulk, bulk[:, TILE:]], axis=1).astype(BF)
    bulk = bulk.reshape(NP, count // NP * slots, TILE)

    back = swap_prow(message)
    last, message = lower_call(1, pos, back, bases[1], [], pack_all)
    back = swap_prow(jnp.concatenate([message, bulk], axis=1))
    bulk = total(back[:, ROWS:]).astype(BF)
    middle, message = lower_call(0, pos, back[:, :ROWS], bases[0], [last], pack_all)
    back = swap_prow(jnp.concatenate([message, to_all(bulk, NP)], axis=1))
    bulk = back[:, ROWS:].reshape(count, width).astype(F32)
    first = total(back[:, :ROWS]).astype(BF)

    window = jnp.concatenate([first, middle, last], axis=0)
    window = window.reshape(STEPS, rows_own, PER, TILE).transpose(0, 2, 1, 3)
    window = swap_pcol(choose(window.reshape(STEPS * PER, rows_own, TILE), first_tiles))
    window = window.reshape(count, TILE).astype(F32)
    slot_solution = jnp.where(my_block < STEPS, window, solved[:, :TILE])
    backward = jnp.concatenate([slot_solution, solved[:, TILE:]], axis=1)
    state0 = jnp.take(rhs, local_pivots, axis=1)
    slot_forward = jnp.where(my_block < STEPS, bulk[:, :TILE], state0[:, :TILE] - bulk[:, :TILE])
    forward = jnp.concatenate([slot_forward, state0[:, TILE:] - bulk[:, TILE:]], axis=1)
    return (forward, backward)


def solution(mesh):
    return jax.shard_map(
        body,
        mesh=mesh,
        in_specs=(
            P(None, "pcol"),
            P("pcol"),
            P(),
            P(None, "prow", "pcol"),
            P(None, "pcol", "prow"),
            P(None, "prow", "pcol"),
            P(None, "prow", "pcol"),
            P(None, "pcol"),
        ),
        out_specs=(P(None, "pcol"), P(None, "pcol")),
        check_vma=False,
    )
```

```python
import jax
import jax.numpy as jnp
from jax import lax
from jax.experimental import pallas as pl
from jax.experimental.pallas import tpu as pltpu
from jax.sharding import PartitionSpec as P

NB = 2048
TILE = 256
STEPS = 3
NY = 4
NZ = 8
NP = 8
NC = 32
PER = NB // TILE
PIECE = NB // NC
Y_GROUPS = [[z * NY + y for y in range(NY)] for z in range(NZ)]
Z_GROUPS = [[z * NY + y for z in range(NZ)] for y in range(NY)]
BF = jnp.bfloat16
F32 = jnp.float32
UPPER_AT = STEPS * PIECE
LOWER_AT = UPPER_AT + PIECE
PACK = LOWER_AT + (STEPS - 1) * TILE
ROWS = 16


def swap_y(x):
    return lax.all_to_all(x, "pcol", 0, 0, axis_index_groups=Y_GROUPS, tiled=True)


def pass_y(x, step):
    return lax.ppermute(x, "pcol", [(at, at ^ step) for at in range(NC)])


def swap_z(x):
    return lax.all_to_all(x, "pcol", 0, 0, axis_index_groups=Z_GROUPS, tiled=True)


def swap_pcol(x):
    return lax.all_to_all(x, "pcol", 0, 0, tiled=True)


def swap_prow(x):
    return lax.all_to_all(x, "prow", 0, 0, tiled=True)


def to_all(x, count):
    return jnp.broadcast_to(x[None], (count,) + x.shape)


def total(x):
    return jnp.sum(x.astype(F32), axis=0)


def choose(values, index):
    where = (index[:, None] == jnp.arange(values.shape[0])[None, :]).astype(BF)
    flat = jnp.dot(where, values.reshape(values.shape[0], -1), preferred_element_type=F32)
    return flat.astype(BF).reshape((index.shape[0],) + values.shape[1:])


def dot_nt(a, b):
    return lax.dot_general(a, b, (((1,), (1,)), ((), ())), preferred_element_type=F32)


def dot_nn(a, b):
    return jnp.dot(a, b, preferred_element_type=F32)


def place_mask(place):
    return lax.broadcasted_iota(jnp.int32, (ROWS, TILE), 0) % PER == place


def lower_part(resid, inverse):
    full = dot_nt(resid, inverse[...].reshape(NB, TILE))
    part = full[:, :TILE]
    for place in range(1, PER):
        part = jnp.where(place_mask(place), full[:, place * TILE : (place + 1) * TILE], part)
    return part.astype(BF)


def last_kernel(pos, got, pick_own, outer, pack, solved_out, message_out, upper, inverse, sems):
    copies = [
        pltpu.make_async_copy(pack.at[:, pl.ds(UPPER_AT, PIECE), :], upper, sems.at[0]),
        pltpu.make_async_copy(
            pack.at[:, pl.ds((STEPS - 1) * PIECE, PIECE), :], inverse, sems.at[1]
        ),
    ]
    for copy in copies:
        copy.start()
    copies[0].wait()
    block = jnp.concatenate([got[pos[place]] for place in range(PER)], axis=1)
    value = dot_nn(block, upper[...].reshape(NB, TILE)).astype(BF)
    solved_out[...] = value
    resid = (dot_nn(pick_own[...], value) - outer[...]).astype(BF)
    copies[1].wait()
    part = lower_part(resid, inverse)
    for index in range(NP):
        message_out[index] = part


def last_call(pos, got, pick_own, outer, pack):
    vmem = pl.BlockSpec(memory_space=pltpu.VMEM)
    return pl.pallas_call(
        last_kernel,
        out_shape=(
            jax.ShapeDtypeStruct((ROWS, TILE), BF),
            jax.ShapeDtypeStruct((NP, ROWS, TILE), BF),
        ),
        in_specs=[
            pl.BlockSpec(memory_space=pltpu.SMEM),
            vmem,
            vmem,
            vmem,
            pl.BlockSpec(memory_space=pltpu.HBM),
        ],
        out_specs=(vmem, vmem),
        scratch_shapes=[
            pltpu.VMEM((NC, PIECE, TILE), BF),
            pltpu.VMEM((NC, PIECE, TILE), BF),
            pltpu.SemaphoreType.DMA((2,)),
        ],
        compiler_params=pltpu.CompilerParams(vmem_limit_bytes=24 << 20),
        name="last_block",
    )(pos, got, pick_own, outer, pack)


def lower_kernel(step, pos, back, base, *rest):
    known = rest[: STEPS - 2 - step]
    pack, value_out, message_out, tiles, inverse, sems = rest[STEPS - 2 - step :]
    later = list(range(step + 1, STEPS))
    first = pltpu.make_async_copy(
        pack.at[:, pl.ds(step * PIECE, PIECE), :], inverse, sems.at[len(later) * PER]
    )
    copies = []
    for at, block in enumerate(later):
        for place in range(PER):
            slot = at * PER + place
            copy = pltpu.make_async_copy(
                pack.at[pos[block * PER + place], pl.ds(LOWER_AT + step * TILE, TILE), :],
                tiles.at[at, :, pl.ds(place * TILE, TILE)],
                sems.at[slot],
            )
            copy.start()
            copies.append(copy)
    first.start()
    value = jnp.sum(back[...].astype(F32), axis=0).astype(BF)
    value_out[...] = value
    sums = jnp.zeros((ROWS, TILE), F32)
    for at in reversed(range(len(later))):
        solved = value if at == 0 else known[at - 1][...]
        wide = jnp.concatenate(
            [jnp.where(place_mask(place), solved, jnp.zeros_like(solved)) for place in range(PER)],
            axis=1,
        )
        for place in range(PER):
            copies[at * PER + place].wait()
        sums = sums + dot_nt(wide, tiles[at])
    sums = jnp.sum(sums.reshape(ROWS // PER, PER, TILE), axis=1, keepdims=True)
    sums = jnp.broadcast_to(sums, (ROWS // PER, PER, TILE)).reshape(ROWS, TILE)
    resid = (base[...] - sums).astype(BF)
    first.wait()
    part = lower_part(resid, inverse)
    for index in range(NP):
        message_out[index] = part


def lower_call(step, pos, back, base, known, pack):
    vmem = pl.BlockSpec(memory_space=pltpu.VMEM)
    later = STEPS - 1 - step
    count = later * PER
    return pl.pallas_call(
        lambda *refs: lower_kernel(step, *refs),
        out_shape=(
            jax.ShapeDtypeStruct((ROWS, TILE), BF),
            jax.ShapeDtypeStruct((NP, ROWS, TILE), BF),
        ),
        in_specs=[pl.BlockSpec(memory_space=pltpu.SMEM), vmem, vmem]
        + [vmem] * len(known)
        + [pl.BlockSpec(memory_space=pltpu.HBM)],
        out_specs=(vmem, vmem),
        scratch_shapes=[
            pltpu.VMEM((later, TILE, NB), BF),
            pltpu.VMEM((NC, PIECE, TILE), BF),
            pltpu.SemaphoreType.DMA((count + 1,)),
        ],
        compiler_params=pltpu.CompilerParams(vmem_limit_bytes=24 << 20),
        name=f"lower_block_{step}",
    )(pos, back, base, *known, pack)


def body(rhs, pivots, tile_of, upper_rows, upper_inv, lower_rows, lower_inv, solved):
    col = lax.axis_index("pcol")
    row = lax.axis_index("prow")
    z = col // NY
    y = col % NY
    count, width = rhs.shape
    slots = width // TILE
    rows_z = count // NY
    rows_own = count // NC
    first_tiles = tile_of.reshape(NC, slots)[:, 0]
    my_tile = first_tiles[col]
    my_block = my_tile // PER
    my_place = my_tile % PER
    plane_tiles = jnp.stack([first_tiles[z * NY + (y ^ step)] for step in range(NY)])
    plane_blocks = plane_tiles // PER
    pos = jnp.sum(
        jnp.where(
            first_tiles[None, :] == jnp.arange(STEPS * PER)[:, None],
            jnp.arange(NC, dtype=jnp.int32)[None, :],
            0,
        ),
        axis=1,
        dtype=jnp.int32,
    )

    pack = jnp.concatenate(
        [
            jnp.swapaxes(lower_inv, 1, 2).reshape(STEPS * PIECE, TILE),
            upper_inv[STEPS - 1],
            lower_rows[: STEPS - 1, :, :TILE].reshape((STEPS - 1) * TILE, TILE),
        ],
        axis=0,
    )
    pack_all = lax.all_gather(pack, "pcol", axis=0)

    local_pivots = pivots - col * width
    own = jnp.take(rhs[:, :TILE], local_pivots[:TILE], axis=1)
    own = own.reshape(NZ, NY, rows_own, TILE).transpose(1, 0, 2, 3).reshape(NY, rows_z, TILE)
    own_high = own.astype(BF)
    own_low = (own - own_high.astype(F32)).astype(BF)
    first_inverses = upper_inv[: STEPS - 1].reshape((STEPS - 1) * PIECE, TILE)
    got = swap_y(jnp.concatenate([own_high, own_low, to_all(first_inverses, NY)], axis=1))
    tiles = got[:, :rows_z].astype(F32) + got[:, rows_z : 2 * rows_z].astype(F32)
    tiles = jnp.stack(
        [lax.dynamic_index_in_dim(tiles, y ^ step, 0, False) for step in range(NY)]
    )
    inverse = []
    for step in range(STEPS - 1):
        start = 2 * rows_z + step * PIECE
        inverse.append(got[:, start : start + PIECE].reshape(TILE, TILE))

    slot_known = jnp.where(my_block >= STEPS, solved[:, :TILE], 0.0)
    known = jnp.concatenate([slot_known, solved[:, TILE:]], axis=1).astype(BF)
    outer = lax.dot_general(
        known, lower_rows, (((1,), (2,)), ((), ())), preferred_element_type=F32
    )
    outer = outer.astype(BF).reshape(NZ, NY, rows_own, STEPS, TILE).transpose(1, 0, 2, 3, 4)
    outer = outer.reshape(NY, NZ * rows_own * STEPS, TILE)
    upper_pack = upper_rows[: STEPS - 1, :, :TILE].reshape((STEPS - 1) * TILE, TILE)
    near = [upper_pack]
    outer_sum = lax.dynamic_index_in_dim(outer, y, 0, False).astype(F32)
    for step in range(1, NY):
        theirs = lax.dynamic_index_in_dim(outer, y ^ step, 0, False)
        got = pass_y(jnp.concatenate([upper_pack, theirs], axis=0), step)
        near.append(got[: (STEPS - 1) * TILE])
        outer_sum = outer_sum + got[(STEPS - 1) * TILE :].astype(F32)
    upper_tiles = [
        jnp.stack([part[step * TILE : (step + 1) * TILE] for part in near])
        for step in range(STEPS - 1)
    ]
    outer = outer_sum.astype(BF).reshape(NZ, rows_own * STEPS, TILE)

    finished = []
    for step in range(STEPS - 1):
        block = tiles.astype(BF)
        pick = plane_tiles[None, :] == step * PER + jnp.arange(NZ)[:, None]
        routed = jnp.sum(jnp.where(pick[:, :, None, None], block[None], 0), axis=1)
        mine = jnp.sum(swap_z(routed), axis=0)
        part = jnp.dot(mine, inverse[step], preferred_element_type=F32).astype(BF)
        message = to_all(part, NZ)
        if step == 1:
            message = jnp.concatenate([message, outer], axis=1)
        back = total(swap_z(message))
        solved_rows = back[:rows_z].astype(BF)
        if step == 1:
            outer = back[rows_z:].reshape(rows_own, STEPS, TILE)
        finished.append(solved_rows)
        update = lax.dot_general(
            solved_rows, upper_tiles[step], (((1,), (1,)), ((), ())), preferred_element_type=F32
        )
        update = total(swap_prow(to_all(update.astype(BF), NP)))
        update = update.transpose(1, 0, 2)
        tiles = tiles - jnp.where((plane_blocks > step)[:, None, None], update, 0.0)

    got = swap_z(to_all(tiles.astype(BF), NZ).reshape(NZ * NY, rows_z, TILE))
    order = jnp.arange(ROWS)
    pick_own = (
        (order[None, :] // rows_own == z) & (order[None, :] % rows_own == order[:, None] // PER)
    ).astype(BF)
    outer = jnp.repeat(outer.transpose(1, 0, 2), PER, axis=1)
    last_pos = pos[(STEPS - 1) * PER :]
    last_pos = last_pos - last_pos % NY + ((last_pos % NY) ^ y)
    last, message = last_call(last_pos, got, pick_own, outer[STEPS - 1], pack_all)
    finished.append(last)
    bases = [
        jnp.dot(pick_own, finished[step], preferred_element_type=F32) - outer[step]
        for step in range(STEPS - 1)
    ]

    stacked, message = lax.optimization_barrier((jnp.concatenate(finished, axis=0), message))
    every = swap_y(to_all(stacked, NY)).reshape(NY, STEPS, NZ, rows_own, TILE)
    every = every.transpose(1, 2, 0, 3, 4).reshape(STEPS, count, TILE)
    bulk = jnp.dot(
        jnp.concatenate(list(every), axis=1),
        upper_rows.reshape(STEPS * TILE, width),
        preferred_element_type=F32,
    )
    window_value = jnp.where(
        my_place == row, lax.dynamic_index_in_dim(every, jnp.minimum(my_block, STEPS - 1), 0, False), 0
    ).astype(F32)
    slot_bulk = jnp.where(my_block < STEPS, window_value, bulk[:, :TILE])
    bulk = jnp.concatenate([slot_bulk, bulk[:, TILE:]], axis=1).astype(BF)
    bulk = bulk.reshape(NP, count // NP * slots, TILE)

    back = swap_prow(message)
    last, message = lower_call(1, pos, back, bases[1], [], pack_all)
    back = swap_prow(jnp.concatenate([message, bulk], axis=1))
    bulk = total(back[:, ROWS:]).astype(BF)
    middle, message = lower_call(0, pos, back[:, :ROWS], bases[0], [last], pack_all)
    back = swap_prow(jnp.concatenate([message, to_all(bulk, NP)], axis=1))
    bulk = back[:, ROWS:].reshape(count, width).astype(F32)
    first = total(back[:, :ROWS]).astype(BF)

    window = jnp.concatenate([first, middle, last], axis=0)
    window = window.reshape(STEPS, rows_own, PER, TILE).transpose(0, 2, 1, 3)
    window = swap_pcol(choose(window.reshape(STEPS * PER, rows_own, TILE), first_tiles))
    window = window.reshape(count, TILE).astype(F32)
    slot_solution = jnp.where(my_block < STEPS, window, solved[:, :TILE])
    backward = jnp.concatenate([slot_solution, solved[:, TILE:]], axis=1)
    state0 = jnp.take(rhs, local_pivots, axis=1)
    slot_forward = jnp.where(my_block < STEPS, bulk[:, :TILE], state0[:, :TILE] - bulk[:, :TILE])
    forward = jnp.concatenate([slot_forward, state0[:, TILE:] - bulk[:, TILE:]], axis=1)
    return (forward, backward)


def solution(mesh):
    return jax.shard_map(
        body,
        mesh=mesh,
        in_specs=(
            P(None, "pcol"),
            P("pcol"),
            P(),
            P(None, "prow", "pcol"),
            P(None, "pcol", "prow"),
            P(None, "prow", "pcol"),
            P(None, "prow", "pcol"),
            P(None, "pcol"),
        ),
        out_specs=(P(None, "pcol"), P(None, "pcol")),
        check_vma=False,
    )
```

```python
import jax
import jax.numpy as jnp
from jax import lax
from jax.experimental import pallas as pl
from jax.experimental.pallas import tpu as pltpu
from jax.sharding import PartitionSpec as P

NB = 2048
TILE = 256
STEPS = 3
NY = 4
NZ = 8
NP = 8
NC = 32
PER = NB // TILE
PIECE = NB // NC
Y_GROUPS = [[z * NY + y for y in range(NY)] for z in range(NZ)]
Z_GROUPS = [[z * NY + y for z in range(NZ)] for y in range(NY)]
BF = jnp.bfloat16
F32 = jnp.float32
UPPER_AT = STEPS * PIECE
LOWER_AT = UPPER_AT + PIECE
PACK = LOWER_AT + (STEPS - 1) * TILE
ROWS = 16


def swap_y(x):
    return lax.all_to_all(x, "pcol", 0, 0, axis_index_groups=Y_GROUPS, tiled=True)


def pass_y(x, step):
    return lax.ppermute(x, "pcol", [(at, at ^ step) for at in range(NC)])


def pass_prow(x, step):
    return lax.ppermute(x, "prow", [(at, at ^ step) for at in range(NP)])


def by_place(parts, index, count):
    parts = jnp.stack(parts)
    return jnp.stack(
        [lax.dynamic_index_in_dim(parts, index ^ place, 0, False) for place in range(count)]
    )


def swap_z(x):
    return lax.all_to_all(x, "pcol", 0, 0, axis_index_groups=Z_GROUPS, tiled=True)


def swap_pcol(x):
    return lax.all_to_all(x, "pcol", 0, 0, tiled=True)


def swap_prow(x):
    return lax.all_to_all(x, "prow", 0, 0, tiled=True)


def to_all(x, count):
    return jnp.broadcast_to(x[None], (count,) + x.shape)


def total(x):
    return jnp.sum(x.astype(F32), axis=0)


def choose(values, index):
    where = (index[:, None] == jnp.arange(values.shape[0])[None, :]).astype(BF)
    flat = jnp.dot(where, values.reshape(values.shape[0], -1), preferred_element_type=F32)
    return flat.astype(BF).reshape((index.shape[0],) + values.shape[1:])


def dot_nt(a, b):
    return lax.dot_general(a, b, (((1,), (1,)), ((), ())), preferred_element_type=F32)


def dot_nn(a, b):
    return jnp.dot(a, b, preferred_element_type=F32)


def place_mask(place):
    return lax.broadcasted_iota(jnp.int32, (ROWS, TILE), 0) % PER == place


def lower_part(resid, inverse):
    full = dot_nt(resid, inverse[...].reshape(NB, TILE))
    part = full[:, :TILE]
    for place in range(1, PER):
        part = jnp.where(place_mask(place), full[:, place * TILE : (place + 1) * TILE], part)
    return part.astype(BF)


def last_kernel(pos, got, pick_own, outer, pack, solved_out, message_out, upper, inverse, sems):
    copies = [
        pltpu.make_async_copy(pack.at[:, pl.ds(UPPER_AT, PIECE), :], upper, sems.at[0]),
        pltpu.make_async_copy(
            pack.at[:, pl.ds((STEPS - 1) * PIECE, PIECE), :], inverse, sems.at[1]
        ),
    ]
    for copy in copies:
        copy.start()
    copies[0].wait()
    block = jnp.concatenate([got[pos[place]] for place in range(PER)], axis=1)
    value = dot_nn(block, upper[...].reshape(NB, TILE)).astype(BF)
    solved_out[...] = value
    resid = (dot_nn(pick_own[...], value) - outer[...]).astype(BF)
    copies[1].wait()
    part = lower_part(resid, inverse)
    for index in range(NP):
        message_out[index] = part


def last_call(pos, got, pick_own, outer, pack):
    vmem = pl.BlockSpec(memory_space=pltpu.VMEM)
    return pl.pallas_call(
        last_kernel,
        out_shape=(
            jax.ShapeDtypeStruct((ROWS, TILE), BF),
            jax.ShapeDtypeStruct((NP, ROWS, TILE), BF),
        ),
        in_specs=[
            pl.BlockSpec(memory_space=pltpu.SMEM),
            vmem,
            vmem,
            vmem,
            pl.BlockSpec(memory_space=pltpu.HBM),
        ],
        out_specs=(vmem, vmem),
        scratch_shapes=[
            pltpu.VMEM((NC, PIECE, TILE), BF),
            pltpu.VMEM((NC, PIECE, TILE), BF),
            pltpu.SemaphoreType.DMA((2,)),
        ],
        compiler_params=pltpu.CompilerParams(vmem_limit_bytes=50 << 20),
        name="last_block",
    )(pos, got, pick_own, outer, pack)


def lower_kernel(step, pos, back, base, *rest):
    known = rest[: STEPS - 2 - step]
    pack, value_out, message_out, tiles, inverse, sems = rest[STEPS - 2 - step :]
    later = list(range(step + 1, STEPS))
    first = pltpu.make_async_copy(
        pack.at[:, pl.ds(step * PIECE, PIECE), :], inverse, sems.at[len(later) * PER]
    )
    copies = []
    for at, block in enumerate(later):
        for place in range(PER):
            slot = at * PER + place
            copy = pltpu.make_async_copy(
                pack.at[pos[block * PER + place], pl.ds(LOWER_AT + step * TILE, TILE), :],
                tiles.at[at, :, pl.ds(place * TILE, TILE)],
                sems.at[slot],
            )
            copy.start()
            copies.append(copy)
    first.start()
    value = jnp.sum(back[...].astype(F32), axis=0).astype(BF)
    value_out[...] = value
    sums = jnp.zeros((ROWS, TILE), F32)
    for at in reversed(range(len(later))):
        solved = value if at == 0 else known[at - 1][...]
        wide = jnp.concatenate(
            [jnp.where(place_mask(place), solved, jnp.zeros_like(solved)) for place in range(PER)],
            axis=1,
        )
        for place in range(PER):
            copies[at * PER + place].wait()
        sums = sums + dot_nt(wide, tiles[at])
    sums = jnp.sum(sums.reshape(ROWS // PER, PER, TILE), axis=1, keepdims=True)
    sums = jnp.broadcast_to(sums, (ROWS // PER, PER, TILE)).reshape(ROWS, TILE)
    resid = (base[...] - sums).astype(BF)
    first.wait()
    part = lower_part(resid, inverse)
    for index in range(NP):
        message_out[index] = part


def lower_call(step, pos, back, base, known, pack):
    vmem = pl.BlockSpec(memory_space=pltpu.VMEM)
    later = STEPS - 1 - step
    count = later * PER
    return pl.pallas_call(
        lambda *refs: lower_kernel(step, *refs),
        out_shape=(
            jax.ShapeDtypeStruct((ROWS, TILE), BF),
            jax.ShapeDtypeStruct((NP, ROWS, TILE), BF),
        ),
        in_specs=[pl.BlockSpec(memory_space=pltpu.SMEM), vmem, vmem]
        + [vmem] * len(known)
        + [pl.BlockSpec(memory_space=pltpu.HBM)],
        out_specs=(vmem, vmem),
        scratch_shapes=[
            pltpu.VMEM((later, TILE, NB), BF),
            pltpu.VMEM((NC, PIECE, TILE), BF),
            pltpu.SemaphoreType.DMA((count + 1,)),
        ],
        compiler_params=pltpu.CompilerParams(vmem_limit_bytes=50 << 20),
        name=f"lower_block_{step}",
    )(pos, back, base, *known, pack)


def body(rhs, pivots, tile_of, upper_rows, upper_inv, lower_rows, lower_inv, solved):
    col = lax.axis_index("pcol")
    row = lax.axis_index("prow")
    z = col // NY
    y = col % NY
    count, width = rhs.shape
    slots = width // TILE
    rows_z = count // NY
    rows_own = count // NC
    first_tiles = tile_of.reshape(NC, slots)[:, 0]
    my_tile = first_tiles[col]
    my_block = my_tile // PER
    my_place = my_tile % PER
    plane_tiles = jnp.stack([first_tiles[z * NY + (y ^ step)] for step in range(NY)])
    plane_blocks = plane_tiles // PER
    pos = jnp.sum(
        jnp.where(
            first_tiles[None, :] == jnp.arange(STEPS * PER)[:, None],
            jnp.arange(NC, dtype=jnp.int32)[None, :],
            0,
        ),
        axis=1,
        dtype=jnp.int32,
    )

    pack = jnp.concatenate(
        [
            jnp.swapaxes(lower_inv, 1, 2).reshape(STEPS * PIECE, TILE),
            upper_inv[STEPS - 1],
            lower_rows[: STEPS - 1, :, :TILE].reshape((STEPS - 1) * TILE, TILE),
        ],
        axis=0,
    )
    pack_all = lax.all_gather(pack, "pcol", axis=0)

    local_pivots = pivots - col * width
    own = jnp.take(rhs[:, :TILE], local_pivots[:TILE], axis=1)
    own = own.reshape(NZ, NY, rows_own, TILE).transpose(1, 0, 2, 3).reshape(NY, rows_z, TILE)
    own_high = own.astype(BF)
    own_low = (own - own_high.astype(F32)).astype(BF)
    first_inverses = upper_inv[: STEPS - 1].reshape((STEPS - 1) * PIECE, TILE)
    got = swap_y(jnp.concatenate([own_high, own_low, to_all(first_inverses, NY)], axis=1))
    tiles = got[:, :rows_z].astype(F32) + got[:, rows_z : 2 * rows_z].astype(F32)
    tiles = jnp.stack(
        [lax.dynamic_index_in_dim(tiles, y ^ step, 0, False) for step in range(NY)]
    )
    inverse = []
    for step in range(STEPS - 1):
        start = 2 * rows_z + step * PIECE
        inverse.append(got[:, start : start + PIECE].reshape(TILE, TILE))

    upper_pack = upper_rows[: STEPS - 1, :, :TILE].reshape((STEPS - 1) * TILE, TILE)
    near = [upper_pack] + [pass_y(upper_pack, step) for step in range(1, NY)]
    upper_tiles = [
        jnp.stack([part[step * TILE : (step + 1) * TILE] for part in near])
        for step in range(STEPS - 1)
    ]

    finished = []
    for step in range(STEPS - 1):
        block = tiles.astype(BF)
        pick = plane_tiles[None, :] == step * PER + jnp.arange(NZ)[:, None]
        routed = jnp.sum(jnp.where(pick[:, :, None, None], block[None], 0), axis=1)
        if step == 0:
            routed, solved_now = lax.optimization_barrier((routed, solved))
        if step == 1:
            routed, rhs_now = lax.optimization_barrier((routed, rhs))
            state0 = jnp.take(rhs_now, local_pivots, axis=1)
        mine = jnp.sum(swap_z(routed), axis=0)
        part = jnp.dot(mine, inverse[step], preferred_element_type=F32).astype(BF)
        message = to_all(part, NZ)
        if step == 0:
            slot_known = jnp.where(my_block >= STEPS, solved_now[:, :TILE], 0.0)
            known = jnp.concatenate([slot_known, solved_now[:, TILE:]], axis=1).astype(BF)
            outer = lax.dot_general(
                known, lower_rows, (((1,), (2,)), ((), ())), preferred_element_type=F32
            )
            outer = outer.astype(BF).reshape(NZ, NY, rows_own, STEPS, TILE)
            outer = outer.transpose(1, 0, 2, 3, 4).reshape(NY, NZ * rows_own * STEPS, TILE)
            outer_sum = lax.dynamic_index_in_dim(outer, y, 0, False).astype(F32)
            for other in range(1, NY):
                theirs = lax.dynamic_index_in_dim(outer, y ^ other, 0, False)
                outer_sum = outer_sum + pass_y(theirs, other).astype(F32)
            outer = outer_sum.astype(BF).reshape(NZ, rows_own * STEPS, TILE)
        if step == 1:
            message = jnp.concatenate([message, outer], axis=1)
        back = total(swap_z(message))
        solved_rows = back[:rows_z].astype(BF)
        if step == 1:
            outer = back[rows_z:].reshape(rows_own, STEPS, TILE)
        finished.append(solved_rows)
        update = lax.dot_general(
            solved_rows, upper_tiles[step], (((1,), (1,)), ((), ())), preferred_element_type=F32
        )
        update = total(swap_prow(to_all(update.astype(BF), NP)))
        update = update.transpose(1, 0, 2)
        tiles = tiles - jnp.where((plane_blocks > step)[:, None, None], update, 0.0)

    got = swap_z(to_all(tiles.astype(BF), NZ).reshape(NZ * NY, rows_z, TILE))
    order = jnp.arange(ROWS)
    pick_own = (
        (order[None, :] // rows_own == z) & (order[None, :] % rows_own == order[:, None] // PER)
    ).astype(BF)
    outer = jnp.repeat(outer.transpose(1, 0, 2), PER, axis=1)
    last_pos = pos[(STEPS - 1) * PER :]
    last_pos = last_pos - last_pos % NY + ((last_pos % NY) ^ y)
    last, message = last_call(last_pos, got, pick_own, outer[STEPS - 1], pack_all)
    finished.append(last)
    bases = [
        jnp.dot(pick_own, finished[step], preferred_element_type=F32) - outer[step]
        for step in range(STEPS - 1)
    ]

    stacked, message = lax.optimization_barrier((jnp.concatenate(finished, axis=0), message))
    every = [stacked] + [pass_y(stacked, step) for step in range(1, NY)]
    back = swap_prow(message)
    last, message = lower_call(1, pos, back, bases[1], [], pack_all)
    message, every = lax.optimization_barrier((message, every))
    every = by_place(every, y, NY).reshape(NY, STEPS, NZ, rows_own, TILE)
    every = every.transpose(1, 2, 0, 3, 4).reshape(STEPS, count, TILE)
    bulk = jnp.dot(
        jnp.concatenate(list(every), axis=1),
        upper_rows.reshape(STEPS * TILE, width),
        preferred_element_type=F32,
    )
    window_value = jnp.where(
        my_place == row, lax.dynamic_index_in_dim(every, jnp.minimum(my_block, STEPS - 1), 0, False), 0
    ).astype(F32)
    slot_bulk = jnp.where(my_block < STEPS, window_value, bulk[:, :TILE])
    bulk = jnp.concatenate([slot_bulk, bulk[:, TILE:]], axis=1).astype(BF)
    bulk = bulk.reshape(NP, count // NP * slots, TILE)

    back = swap_prow(message)
    middle, message = lower_call(0, pos, back, bases[0], [last], pack_all)
    back = swap_prow(jnp.concatenate([message, bulk], axis=1))
    first = total(back[:, :ROWS]).astype(BF)

    window = jnp.concatenate([first, middle, last], axis=0)
    window = window.reshape(STEPS, rows_own, PER, TILE).transpose(0, 2, 1, 3)
    window = choose(window.reshape(STEPS * PER, rows_own, TILE), first_tiles)
    bulk = total(back[:, ROWS:]).astype(BF)
    window, bulk = lax.optimization_barrier((window, bulk))
    window = swap_pcol(window)
    pair = jnp.stack([bulk, pass_prow(bulk, 1)])
    pairs = [pair] + [pass_prow(pair, step) for step in range(2, NP, 2)]
    bulk = by_place([part[side] for part in pairs for side in range(2)], row, NP)
    bulk = bulk.reshape(count, width).astype(F32)
    slot_forward = jnp.where(my_block < STEPS, bulk[:, :TILE], state0[:, :TILE] - bulk[:, :TILE])
    forward = jnp.concatenate([slot_forward, state0[:, TILE:] - bulk[:, TILE:]], axis=1)
    forward, window = lax.optimization_barrier((forward, window))
    window = window.reshape(count, TILE).astype(F32)
    slot_solution = jnp.where(my_block < STEPS, window, solved[:, :TILE])
    backward = jnp.concatenate([slot_solution, solved[:, TILE:]], axis=1)
    return (forward, backward)


def solution(mesh):
    return jax.shard_map(
        body,
        mesh=mesh,
        in_specs=(
            P(None, "pcol"),
            P("pcol"),
            P(),
            P(None, "prow", "pcol"),
            P(None, "pcol", "prow"),
            P(None, "prow", "pcol"),
            P(None, "prow", "pcol"),
            P(None, "pcol"),
        ),
        out_specs=(P(None, "pcol"), P(None, "pcol")),
        check_vma=False,
    )
```

```python
import jax
import jax.numpy as jnp
from jax import lax
from jax.experimental import pallas as pl
from jax.experimental.pallas import tpu as pltpu
from jax.sharding import PartitionSpec as P

NB = 2048
TILE = 256
STEPS = 3
NY = 4
NZ = 8
NP = 8
NC = 32
PER = NB // TILE
PIECE = NB // NC
Y_GROUPS = [[z * NY + y for y in range(NY)] for z in range(NZ)]
Z_GROUPS = [[z * NY + y for z in range(NZ)] for y in range(NY)]
BF = jnp.bfloat16
F32 = jnp.float32
UPPER_AT = STEPS * PIECE
LOWER_AT = UPPER_AT + PIECE
PACK = LOWER_AT + (STEPS - 1) * TILE
ROWS = 16
GRANT = 49 << 20
VMEM = pl.BlockSpec(memory_space=pltpu.VMEM)
SMEM = pl.BlockSpec(memory_space=pltpu.SMEM)
HBM = pl.BlockSpec(memory_space=pltpu.HBM)


def swap_y(x):
    return lax.all_to_all(x, "pcol", 0, 0, axis_index_groups=Y_GROUPS, tiled=True)


def pass_y(x, step):
    return lax.ppermute(x, "pcol", [(at, at ^ step) for at in range(NC)])


def pass_prow(x, step):
    return lax.ppermute(x, "prow", [(at, at ^ step) for at in range(NP)])


def by_place(parts, index, count):
    parts = jnp.stack(parts)
    return jnp.stack(
        [lax.dynamic_index_in_dim(parts, index ^ place, 0, False) for place in range(count)]
    )


def swap_z(x):
    return lax.all_to_all(x, "pcol", 0, 0, axis_index_groups=Z_GROUPS, tiled=True)


def swap_pcol(x):
    return lax.all_to_all(x, "pcol", 0, 0, tiled=True)


def swap_prow(x):
    return lax.all_to_all(x, "prow", 0, 0, tiled=True)


def to_all(x, count):
    return jnp.broadcast_to(x[None], (count,) + x.shape)


def total(x):
    return jnp.sum(x.astype(F32), axis=0)


def choose(values, index):
    where = (index[:, None] == jnp.arange(values.shape[0])[None, :]).astype(BF)
    flat = jnp.dot(where, values.reshape(values.shape[0], -1), preferred_element_type=F32)
    return flat.astype(BF).reshape((index.shape[0],) + values.shape[1:])


def dot_nt(a, b):
    return lax.dot_general(a, b, (((1,), (1,)), ((), ())), preferred_element_type=F32)


def dot_nn(a, b):
    return jnp.dot(a, b, preferred_element_type=F32)


def place_mask(place):
    return lax.broadcasted_iota(jnp.int32, (ROWS, TILE), 0) % PER == place


def lower_part(resid, inverse):
    full = dot_nt(resid, inverse[...].reshape(NB, TILE))
    part = full[:, :TILE]
    for place in range(1, PER):
        part = jnp.where(place_mask(place), full[:, place * TILE : (place + 1) * TILE], part)
    return part.astype(BF)


def last_kernel(pos, got, pick_own, outer, pack, solved_out, message_out, upper, inverse, sems):
    copies = [
        pltpu.make_async_copy(pack.at[:, pl.ds(UPPER_AT, PIECE), :], upper, sems.at[0]),
        pltpu.make_async_copy(
            pack.at[:, pl.ds((STEPS - 1) * PIECE, PIECE), :], inverse, sems.at[1]
        ),
    ]
    for copy in copies:
        copy.start()
    copies[0].wait()
    _, y = plane()
    block = []
    for place in range(PER):
        at = pos[(STEPS - 1) * PER + place]
        block.append(got[at - at % NY + ((at % NY) ^ y)])
    block = jnp.concatenate(block, axis=1)
    value = dot_nn(block, upper[...].reshape(NB, TILE)).astype(BF)
    solved_out[...] = value
    resid = (dot_nn(pick_own[...], value) - outer[...]).astype(BF)
    copies[1].wait()
    part = lower_part(resid, inverse)
    for index in range(NP):
        message_out[index] = part


def last_call(pos, got, pick_own, outer, pack):
    vmem = pl.BlockSpec(memory_space=pltpu.VMEM)
    return pl.pallas_call(
        last_kernel,
        out_shape=(
            jax.ShapeDtypeStruct((ROWS, TILE), BF),
            jax.ShapeDtypeStruct((NP, ROWS, TILE), BF),
        ),
        in_specs=[
            pl.BlockSpec(memory_space=pltpu.SMEM),
            vmem,
            vmem,
            vmem,
            pl.BlockSpec(memory_space=pltpu.HBM),
        ],
        out_specs=(vmem, vmem),
        scratch_shapes=[
            pltpu.VMEM((NC, PIECE, TILE), BF),
            pltpu.VMEM((NC, PIECE, TILE), BF),
            pltpu.SemaphoreType.DMA((2,)),
        ],
        compiler_params=pltpu.CompilerParams(vmem_limit_bytes=GRANT),
        name="last_block",
    )(pos, got, pick_own, outer, pack)


def call(kernel, name, outs, in_specs, args, scratch=(), out_specs=None, grant=None):
    return pl.pallas_call(
        kernel,
        out_shape=tuple(jax.ShapeDtypeStruct(shape, dtype) for shape, dtype in outs),
        in_specs=in_specs,
        out_specs=tuple(out_specs or [VMEM] * len(outs)),
        scratch_shapes=list(scratch),
        compiler_params=pltpu.CompilerParams(vmem_limit_bytes=grant or 8 << 20),
        name=name,
    )(*args)


def pack_kernel(lower_inverse, upper_inverse, lower, out):
    out[pl.ds(0, UPPER_AT), :] = lower_inverse[...].reshape(UPPER_AT, TILE)
    out[pl.ds(UPPER_AT, PIECE), :] = upper_inverse[0]
    out[pl.ds(LOWER_AT, PACK - LOWER_AT), :] = lower[...].reshape(PACK - LOWER_AT, TILE)


def pos_kernel(tile_of, pos):
    stride = tile_of.shape[0] // NC

    def put(index, carry):
        pos[tile_of[index * stride]] = index
        return carry

    lax.fori_loop(0, NC, put, 0)


def plane():
    col = lax.axis_index("pcol")
    return col // NY, col % NY


def plane_tile(tile_of, z, other):
    return tile_of[(z * NY + other) * (tile_of.shape[0] // NC)]


def first_kernel(tile_of, got, tiles, routed):
    z, y = plane()
    routed[...] = jnp.zeros_like(routed)
    for step in range(NY):
        other = y ^ step
        value = got[other, pl.ds(0, ROWS), :].astype(F32)
        value = value + got[other, pl.ds(ROWS, ROWS), :].astype(F32)
        tiles[step] = value
        tile = plane_tile(tile_of, z, other)

        @pl.when(tile // PER == 0)
        def _():
            routed[tile % PER] = value.astype(BF)


def inverse_kernel(step, back, got, *rest):
    message = rest[-1]
    mine = jnp.sum(back[...].astype(F32), axis=0).astype(BF)
    at = 2 * ROWS + step * PIECE
    weights = jnp.concatenate([got[other, pl.ds(at, PIECE), :] for other in range(NY)], axis=0)
    part = dot_nn(mine, weights).astype(BF)
    for index in range(NZ):
        message[index, pl.ds(0, ROWS), :] = part
        if len(rest) > 1:
            message[index, pl.ds(ROWS, ROWS), :] = rest[0][index]


def update_kernel(step, back, own, near_1, near_2, near_3, solved_out, message, *outer):
    sums = jnp.sum(back[...].astype(F32), axis=0)
    value = sums[:ROWS].astype(BF)
    solved_out[...] = value
    if outer:
        outer[0][...] = sums[ROWS:]
    for index, near in enumerate((own, near_1, near_2, near_3)):
        update = dot_nn(value, near[pl.ds(step * TILE, TILE), :]).astype(BF)
        for other in range(NP):
            message[other, pl.ds(index * ROWS, ROWS), :] = update


def state_kernel(step, tile_of, back, tiles, *outs):
    z, y = plane()
    sums = jnp.sum(back[...].astype(F32), axis=0)
    if step == 0:
        later, routed = outs
        routed[...] = jnp.zeros_like(routed)
    for index in range(NY):
        tile = plane_tile(tile_of, z, y ^ index)
        keep = (tile // PER > step).astype(F32)
        value = tiles[index] - keep * sums[index * ROWS : (index + 1) * ROWS]
        if step == 0:
            later[index] = value

            @pl.when(tile // PER == 1)
            def _():
                routed[tile % PER] = value.astype(BF)

        else:
            for other in range(NZ):
                outs[0][other * NY + index] = value.astype(BF)


def fetch_kernel(step, pos, pack, tiles, inverse, sems):
    copies = [
        pltpu.make_async_copy(
            pack.at[pos[(step + 1 + at) * PER + place], pl.ds(LOWER_AT + step * TILE, TILE), :],
            tiles.at[at, :, pl.ds(place * TILE, TILE)],
            sems.at[at * PER + place],
        )
        for at in range(STEPS - 1 - step)
        for place in range(PER)
    ]
    copies.append(
        pltpu.make_async_copy(
            pack.at[:, pl.ds(step * PIECE, PIECE), :], inverse, sems.at[len(copies)]
        )
    )
    for copy in copies:
        copy.start()
    for copy in copies:
        copy.wait()


def fetch_call(step, pos, pack):
    later = STEPS - 1 - step
    return call(
        lambda *refs: fetch_kernel(step, *refs),
        f"fetch_block_{step}",
        [((later, TILE, NB), BF), ((NC, PIECE, TILE), BF)],
        [SMEM, HBM],
        (pos, pack),
        [pltpu.SemaphoreType.DMA((later * PER + 1,))],
        grant=GRANT,
    )


def lower_kernel(step, back, base, tiles, inverse, *rest):
    known = rest[:-2]
    value_out, message_out = rest[-2:]
    value = jnp.sum(back[...].astype(F32), axis=0).astype(BF)
    value_out[...] = value
    sums = jnp.zeros((ROWS, TILE), F32)
    for at in range(STEPS - 1 - step):
        solved = value if at == 0 else known[at - 1][...]
        wide = jnp.concatenate(
            [jnp.where(place_mask(place), solved, jnp.zeros_like(solved)) for place in range(PER)],
            axis=1,
        )
        sums = sums + dot_nt(wide, tiles[at])
    sums = jnp.sum(sums.reshape(ROWS // PER, PER, TILE), axis=1, keepdims=True)
    sums = jnp.broadcast_to(sums, (ROWS // PER, PER, TILE)).reshape(ROWS, TILE)
    part = lower_part((base[...] - sums).astype(BF), inverse)
    for index in range(NP):
        message_out[index] = part


def lower_call(step, back, base, weights, known):
    return call(
        lambda *refs: lower_kernel(step, *refs),
        f"lower_block_{step}",
        [((ROWS, TILE), BF), ((NP, ROWS, TILE), BF)],
        [VMEM] * (4 + len(known)),
        (back, base, *weights, *known),
        grant=16 << 20,
    )


def body(rhs, pivots, tile_of, upper_rows, upper_inv, lower_rows, lower_inv, solved):
    col = lax.axis_index("pcol")
    row = lax.axis_index("prow")
    z = col // NY
    y = col % NY
    count, width = rhs.shape
    slots = width // TILE
    rows_z = count // NY
    rows_own = count // NC
    first_tiles = tile_of.reshape(NC, slots)[:, 0]
    my_tile = first_tiles[col]
    my_block = my_tile // PER
    my_place = my_tile % PER

    pack = pl.pallas_call(
        pack_kernel,
        out_shape=jax.ShapeDtypeStruct((PACK, TILE), BF),
        grid=(1,),
        in_specs=[
            pl.BlockSpec((STEPS, PIECE, TILE), lambda at: (0, 0, 0)),
            pl.BlockSpec((1, PIECE, TILE), lambda at: (STEPS - 1, 0, 0)),
            pl.BlockSpec((STEPS - 1, TILE, TILE), lambda at: (0, 0, 0)),
        ],
        out_specs=pl.BlockSpec((PACK, TILE), lambda at: (0, 0)),
        compiler_params=pltpu.CompilerParams(vmem_limit_bytes=8 << 20),
        name="pack_window",
    )(jnp.swapaxes(lower_inv, 1, 2), upper_inv, lower_rows)
    pack_all = lax.all_gather(pack, "pcol", axis=0)

    local_pivots = pivots - col * width
    own = jnp.take(rhs[:, :TILE], local_pivots[:TILE], axis=1)
    own = own.reshape(NZ, NY, rows_own, TILE).transpose(1, 0, 2, 3).reshape(NY, rows_z, TILE)
    own_high = own.astype(BF)
    own_low = (own - own_high.astype(F32)).astype(BF)
    first_inverses = upper_inv[: STEPS - 1].reshape((STEPS - 1) * PIECE, TILE)
    start = swap_y(jnp.concatenate([own_high, own_low, to_all(first_inverses, NY)], axis=1))
    tiles, routed = call(
        first_kernel,
        "first_state",
        [((NY, ROWS, TILE), F32), ((NZ, ROWS, TILE), BF)],
        [SMEM, VMEM],
        (tile_of, start),
    )
    upper_pack = upper_rows[: STEPS - 1, :, :TILE].reshape((STEPS - 1) * TILE, TILE)
    near = [upper_pack] + [pass_y(upper_pack, step) for step in range(1, NY)]
    routed, solved_now, tile_now = lax.optimization_barrier((routed, solved, tile_of))
    (pos,) = call(
        pos_kernel, "tile_places", [((NC,), jnp.int32)], [SMEM], (tile_now,), out_specs=[SMEM]
    )

    finished = []
    for step in range(STEPS - 1):
        if step == 1:
            routed, rhs_now = lax.optimization_barrier((routed, rhs))
            state0 = jnp.take(rhs_now, local_pivots, axis=1)
        back = swap_z(routed)
        extra = [outer] if step == 1 else []
        rows = ROWS * (1 + step)
        (message,) = call(
            lambda *refs: inverse_kernel(step, *refs),
            f"inverse_part_{step}",
            [((NZ, rows, TILE), BF)],
            [VMEM] * (2 + len(extra)),
            (back, start, *extra),
        )
        if step == 0:
            slot_known = jnp.where(my_block >= STEPS, solved_now[:, :TILE], 0.0)
            known = jnp.concatenate([slot_known, solved_now[:, TILE:]], axis=1).astype(BF)
            outer = lax.dot_general(
                known, lower_rows, (((1,), (2,)), ((), ())), preferred_element_type=F32
            )
            outer = outer.astype(BF).reshape(NZ, NY, rows_own, STEPS, TILE)
            outer = outer.transpose(1, 0, 2, 3, 4).reshape(NY, NZ * rows_own * STEPS, TILE)
            outer_sum = lax.dynamic_index_in_dim(outer, y, 0, False).astype(F32)
            for other in range(1, NY):
                theirs = lax.dynamic_index_in_dim(outer, y ^ other, 0, False)
                outer_sum = outer_sum + pass_y(theirs, other).astype(F32)
            outer = outer_sum.astype(BF).reshape(NZ, rows_own * STEPS, TILE)
            outer = jnp.pad(outer, ((0, 0), (0, ROWS - rows_own * STEPS), (0, 0)))
        outs = [((ROWS, TILE), BF), ((NP, NY * ROWS, TILE), BF)]
        if step == 1:
            outs.append(((ROWS, TILE), F32))
        value, message, *sums = call(
            lambda *refs: update_kernel(step, *refs),
            f"upper_update_{step}",
            outs,
            [VMEM] * (1 + NY),
            (swap_z(message), *near),
        )
        finished.append(value)
        outs = [((NZ * NY, ROWS, TILE), BF)]
        if step == 0:
            outs = [((NY, ROWS, TILE), F32), ((NZ, ROWS, TILE), BF)]
        found = call(
            lambda *refs: state_kernel(step, *refs),
            f"next_state_{step}",
            outs,
            [SMEM, VMEM, VMEM],
            (tile_of, swap_prow(message), tiles),
        )
        if step == 0:
            tiles, routed = found

    got = swap_z(found[0])
    order = jnp.arange(ROWS)
    pick_own = (
        (order[None, :] // rows_own == z) & (order[None, :] % rows_own == order[:, None] // PER)
    ).astype(BF)
    outer = sums[0][: rows_own * STEPS].reshape(rows_own, STEPS, TILE)
    outer = jnp.repeat(outer.transpose(1, 0, 2), PER, axis=1)
    last, message = last_call(pos, got, pick_own, outer[STEPS - 1], pack_all)
    finished.append(last)
    bases = [
        jnp.dot(pick_own, finished[step], preferred_element_type=F32) - outer[step]
        for step in range(STEPS - 1)
    ]

    message, pos_now = lax.optimization_barrier((message, pos))
    weights = fetch_call(1, pos_now, pack_all)
    back = swap_prow(message)
    last, message = lower_call(1, back, bases[1], weights, [])

    message, stacked, pos_now = lax.optimization_barrier(
        (message, jnp.concatenate(finished, axis=0), pos)
    )
    weights = fetch_call(0, pos_now, pack_all)
    every = [stacked] + [pass_y(stacked, step) for step in range(1, NY)]
    every = by_place(every, y, NY).reshape(NY, STEPS, NZ, rows_own, TILE)
    every = every.transpose(1, 2, 0, 3, 4).reshape(STEPS, count, TILE)
    bulk = jnp.dot(
        jnp.concatenate(list(every), axis=1),
        upper_rows.reshape(STEPS * TILE, width),
        preferred_element_type=F32,
    )
    window_value = jnp.where(
        my_place == row, lax.dynamic_index_in_dim(every, jnp.minimum(my_block, STEPS - 1), 0, False), 0
    ).astype(F32)
    slot_bulk = jnp.where(my_block < STEPS, window_value, bulk[:, :TILE])
    bulk = jnp.concatenate([slot_bulk, bulk[:, TILE:]], axis=1).astype(BF)
    bulk = bulk.reshape(NP, count // NP * slots, TILE)

    back = swap_prow(message)
    middle, message = lower_call(0, back, bases[0], weights, [last])
    back = swap_prow(jnp.concatenate([message, bulk], axis=1))
    first = total(back[:, :ROWS]).astype(BF)

    window = jnp.concatenate([first, middle, last], axis=0)
    window = window.reshape(STEPS, rows_own, PER, TILE).transpose(0, 2, 1, 3)
    window = choose(window.reshape(STEPS * PER, rows_own, TILE), first_tiles)
    bulk = total(back[:, ROWS:]).astype(BF)
    window, bulk = lax.optimization_barrier((window, bulk))
    window = swap_pcol(window)
    pair = jnp.stack([bulk, pass_prow(bulk, 1)])
    pairs = [pair] + [pass_prow(pair, step) for step in range(2, NP, 2)]
    bulk = by_place([part[side] for part in pairs for side in range(2)], row, NP)
    bulk = bulk.reshape(count, width).astype(F32)
    slot_forward = jnp.where(my_block < STEPS, bulk[:, :TILE], state0[:, :TILE] - bulk[:, :TILE])
    forward = jnp.concatenate([slot_forward, state0[:, TILE:] - bulk[:, TILE:]], axis=1)
    forward, window = lax.optimization_barrier((forward, window))
    window = window.reshape(count, TILE).astype(F32)
    slot_solution = jnp.where(my_block < STEPS, window, solved[:, :TILE])
    backward = jnp.concatenate([slot_solution, solved[:, TILE:]], axis=1)
    return (forward, backward)


def solution(mesh):
    return jax.shard_map(
        body,
        mesh=mesh,
        in_specs=(
            P(None, "pcol"),
            P("pcol"),
            P(),
            P(None, "prow", "pcol"),
            P(None, "pcol", "prow"),
            P(None, "prow", "pcol"),
            P(None, "prow", "pcol"),
            P(None, "pcol"),
        ),
        out_specs=(P(None, "pcol"), P(None, "pcol")),
        check_vma=False,
    )
```

```python
import jax
import jax.numpy as jnp
from jax import lax
from jax.experimental import pallas as pl
from jax.experimental.pallas import tpu as pltpu
from jax.sharding import PartitionSpec as P

NB = 2048
TILE = 256
STEPS = 3
NY = 4
NZ = 8
NP = 8
NC = 32
PER = NB // TILE
PIECE = NB // NC
Y_GROUPS = [[z * NY + y for y in range(NY)] for z in range(NZ)]
Z_GROUPS = [[z * NY + y for z in range(NZ)] for y in range(NY)]
BF = jnp.bfloat16
F32 = jnp.float32
UPPER_AT = STEPS * PIECE
LOWER_AT = UPPER_AT + PIECE
PACK = LOWER_AT + (STEPS - 1) * TILE
ROWS = 16
GRANT = 49 << 20
VMEM = pl.BlockSpec(memory_space=pltpu.VMEM)
SMEM = pl.BlockSpec(memory_space=pltpu.SMEM)
HBM = pl.BlockSpec(memory_space=pltpu.HBM)


def swap_y(x):
    return lax.all_to_all(x, "pcol", 0, 0, axis_index_groups=Y_GROUPS, tiled=True)


def pass_y(x, step):
    return lax.ppermute(x, "pcol", [(at, at ^ step) for at in range(NC)])


def pass_prow(x, step):
    return lax.ppermute(x, "prow", [(at, at ^ step) for at in range(NP)])


def by_place(parts, index, count):
    parts = jnp.stack(parts)
    return jnp.stack(
        [lax.dynamic_index_in_dim(parts, index ^ place, 0, False) for place in range(count)]
    )


def swap_z(x):
    return lax.all_to_all(x, "pcol", 0, 0, axis_index_groups=Z_GROUPS, tiled=True)


def swap_pcol(x):
    return lax.all_to_all(x, "pcol", 0, 0, tiled=True)


def swap_prow(x):
    return lax.all_to_all(x, "prow", 0, 0, tiled=True)


def to_all(x, count):
    return jnp.broadcast_to(x[None], (count,) + x.shape)


def total(x):
    return jnp.sum(x.astype(F32), axis=0)


def choose(values, index):
    where = (index[:, None] == jnp.arange(values.shape[0])[None, :]).astype(BF)
    flat = jnp.dot(where, values.reshape(values.shape[0], -1), preferred_element_type=F32)
    return flat.astype(BF).reshape((index.shape[0],) + values.shape[1:])


def dot_nt(a, b):
    return lax.dot_general(a, b, (((1,), (1,)), ((), ())), preferred_element_type=F32)


def dot_nn(a, b):
    return jnp.dot(a, b, preferred_element_type=F32)


def place_mask(place):
    return lax.broadcasted_iota(jnp.int32, (ROWS, TILE), 0) % PER == place


def lower_part(resid, inverse):
    full = dot_nt(resid, inverse[...].reshape(NB, TILE))
    part = full[:, :TILE]
    for place in range(1, PER):
        part = jnp.where(place_mask(place), full[:, place * TILE : (place + 1) * TILE], part)
    return part.astype(BF)


def last_kernel(pos, got, pick_own, outer, pack, solved_out, message_out, upper, inverse, sems):
    copies = [
        pltpu.make_async_copy(pack.at[:, pl.ds(UPPER_AT, PIECE), :], upper, sems.at[0]),
        pltpu.make_async_copy(
            pack.at[:, pl.ds((STEPS - 1) * PIECE, PIECE), :], inverse, sems.at[1]
        ),
    ]
    for copy in copies:
        copy.start()
    copies[0].wait()
    _, y = plane()
    block = []
    for place in range(PER):
        at = pos[(STEPS - 1) * PER + place]
        block.append(got[at - at % NY + ((at % NY) ^ y)])
    block = jnp.concatenate(block, axis=1)
    value = dot_nn(block, upper[...].reshape(NB, TILE)).astype(BF)
    solved_out[...] = value
    resid = (dot_nn(pick_own[...], value) - outer[...]).astype(BF)
    copies[1].wait()
    part = lower_part(resid, inverse)
    for index in range(NP):
        message_out[index] = part


def last_call(pos, got, pick_own, outer, pack):
    vmem = pl.BlockSpec(memory_space=pltpu.VMEM)
    return pl.pallas_call(
        last_kernel,
        out_shape=(
            jax.ShapeDtypeStruct((ROWS, TILE), BF),
            jax.ShapeDtypeStruct((NP, ROWS, TILE), BF),
        ),
        in_specs=[
            pl.BlockSpec(memory_space=pltpu.SMEM),
            vmem,
            vmem,
            vmem,
            pl.BlockSpec(memory_space=pltpu.HBM),
        ],
        out_specs=(vmem, vmem),
        scratch_shapes=[
            pltpu.VMEM((NC, PIECE, TILE), BF),
            pltpu.VMEM((NC, PIECE, TILE), BF),
            pltpu.SemaphoreType.DMA((2,)),
        ],
        compiler_params=pltpu.CompilerParams(vmem_limit_bytes=GRANT),
        name="last_block",
    )(pos, got, pick_own, outer, pack)


def call(kernel, name, outs, in_specs, args, scratch=(), out_specs=None, grant=None):
    return pl.pallas_call(
        kernel,
        out_shape=tuple(jax.ShapeDtypeStruct(shape, dtype) for shape, dtype in outs),
        in_specs=in_specs,
        out_specs=tuple(out_specs or [VMEM] * len(outs)),
        scratch_shapes=list(scratch),
        compiler_params=pltpu.CompilerParams(vmem_limit_bytes=grant or 8 << 20),
        name=name,
    )(*args)


def pos_kernel(tile_of, pos):
    stride = tile_of.shape[0] // NC

    def put(index, carry):
        pos[tile_of[index * stride]] = index
        return carry

    lax.fori_loop(0, NC, put, 0)


def plane():
    col = lax.axis_index("pcol")
    return col // NY, col % NY


def plane_tile(tile_of, z, other):
    return tile_of[(z * NY + other) * (tile_of.shape[0] // NC)]


def first_kernel(tile_of, got, tiles, routed):
    z, y = plane()
    routed[...] = jnp.zeros_like(routed)
    for step in range(NY):
        other = y ^ step
        value = got[other, pl.ds(0, ROWS), :].astype(F32)
        value = value + got[other, pl.ds(ROWS, ROWS), :].astype(F32)
        tiles[step] = value
        tile = plane_tile(tile_of, z, other)

        @pl.when(tile // PER == 0)
        def _():
            routed[tile % PER] = value.astype(BF)


def inverse_kernel(step, back, got, *rest):
    message = rest[-1]
    mine = jnp.sum(back[...].astype(F32), axis=0).astype(BF)
    at = 2 * ROWS + step * PIECE
    weights = jnp.concatenate([got[other, pl.ds(at, PIECE), :] for other in range(NY)], axis=0)
    part = dot_nn(mine, weights).astype(BF)
    for index in range(NZ):
        message[index, pl.ds(0, ROWS), :] = part
        if len(rest) > 1:
            message[index, pl.ds(ROWS, ROWS), :] = rest[0][index]


def update_kernel(step, back, own, near_1, near_2, near_3, solved_out, message, *outer):
    sums = jnp.sum(back[...].astype(F32), axis=0)
    value = sums[:ROWS].astype(BF)
    solved_out[...] = value
    if outer:
        outer[0][...] = sums[ROWS:]
    for index, near in enumerate((own, near_1, near_2, near_3)):
        update = dot_nn(value, near[pl.ds(step * TILE, TILE), :]).astype(BF)
        for other in range(NP):
            message[other, pl.ds(index * ROWS, ROWS), :] = update


def state_kernel(step, tile_of, back, tiles, *outs):
    z, y = plane()
    sums = jnp.sum(back[...].astype(F32), axis=0)
    if step == 0:
        later, routed = outs
        routed[...] = jnp.zeros_like(routed)
    for index in range(NY):
        tile = plane_tile(tile_of, z, y ^ index)
        keep = (tile // PER > step).astype(F32)
        value = tiles[index] - keep * sums[index * ROWS : (index + 1) * ROWS]
        if step == 0:
            later[index] = value

            @pl.when(tile // PER == 1)
            def _():
                routed[tile % PER] = value.astype(BF)

        else:
            for other in range(NZ):
                outs[0][other * NY + index] = value.astype(BF)


def fetch_kernel(step, pos, pack, tiles, inverse, sems):
    copies = [
        pltpu.make_async_copy(
            pack.at[pos[(step + 1 + at) * PER + place], pl.ds(LOWER_AT + step * TILE, TILE), :],
            tiles.at[at, :, pl.ds(place * TILE, TILE)],
            sems.at[at * PER + place],
        )
        for at in range(STEPS - 1 - step)
        for place in range(PER)
    ]
    copies.append(
        pltpu.make_async_copy(
            pack.at[:, pl.ds(step * PIECE, PIECE), :], inverse, sems.at[len(copies)]
        )
    )
    for copy in copies:
        copy.start()
    for copy in copies:
        copy.wait()


def fetch_call(step, pos, pack):
    later = STEPS - 1 - step
    return call(
        lambda *refs: fetch_kernel(step, *refs),
        f"fetch_block_{step}",
        [((later, TILE, NB), BF), ((NC, PIECE, TILE), BF)],
        [SMEM, HBM],
        (pos, pack),
        [pltpu.SemaphoreType.DMA((later * PER + 1,))],
        grant=GRANT,
    )


def lower_kernel(step, back, base, tiles, inverse, *rest):
    known = rest[:-2]
    value_out, message_out = rest[-2:]
    value = jnp.sum(back[...].astype(F32), axis=0).astype(BF)
    value_out[...] = value
    sums = jnp.zeros((ROWS, TILE), F32)
    for at in range(STEPS - 1 - step):
        solved = value if at == 0 else known[at - 1][...]
        wide = jnp.concatenate(
            [jnp.where(place_mask(place), solved, jnp.zeros_like(solved)) for place in range(PER)],
            axis=1,
        )
        sums = sums + dot_nt(wide, tiles[at])
    sums = jnp.sum(sums.reshape(ROWS // PER, PER, TILE), axis=1, keepdims=True)
    sums = jnp.broadcast_to(sums, (ROWS // PER, PER, TILE)).reshape(ROWS, TILE)
    part = lower_part((base[...] - sums).astype(BF), inverse)
    for index in range(NP):
        message_out[index] = part


def lower_call(step, back, base, weights, known):
    return call(
        lambda *refs: lower_kernel(step, *refs),
        f"lower_block_{step}",
        [((ROWS, TILE), BF), ((NP, ROWS, TILE), BF)],
        [VMEM] * (4 + len(known)),
        (back, base, *weights, *known),
        grant=16 << 20,
    )


def body(rhs, pivots, tile_of, upper_rows, upper_inv, lower_rows, lower_inv, solved):
    col = lax.axis_index("pcol")
    row = lax.axis_index("prow")
    z = col // NY
    y = col % NY
    count, width = rhs.shape
    slots = width // TILE
    rows_z = count // NY
    rows_own = count // NC
    first_tiles = tile_of.reshape(NC, slots)[:, 0]
    my_tile = first_tiles[col]
    my_block = my_tile // PER
    my_place = my_tile % PER

    pack = jnp.concatenate(
        [
            jnp.swapaxes(lower_inv, 1, 2).reshape(UPPER_AT, TILE),
            upper_inv[STEPS - 1],
            lower_rows[: STEPS - 1, :, :TILE].reshape(PACK - LOWER_AT, TILE),
        ],
        axis=0,
    )
    pack_all = lax.all_gather(pack, "pcol", axis=0)

    local_pivots = pivots - col * width
    own = jnp.take(rhs[:, :TILE], local_pivots[:TILE], axis=1)
    own = own.reshape(NZ, NY, rows_own, TILE).transpose(1, 0, 2, 3).reshape(NY, rows_z, TILE)
    own_high = own.astype(BF)
    own_low = (own - own_high.astype(F32)).astype(BF)
    first_inverses = upper_inv[: STEPS - 1].reshape((STEPS - 1) * PIECE, TILE)
    start = swap_y(jnp.concatenate([own_high, own_low, to_all(first_inverses, NY)], axis=1))
    tiles, routed = call(
        first_kernel,
        "first_state",
        [((NY, ROWS, TILE), F32), ((NZ, ROWS, TILE), BF)],
        [SMEM, VMEM],
        (tile_of, start),
    )
    upper_pack = upper_rows[: STEPS - 1, :, :TILE].reshape((STEPS - 1) * TILE, TILE)
    near = [upper_pack] + [pass_y(upper_pack, step) for step in range(1, NY)]
    routed, solved_now, tile_now = lax.optimization_barrier((routed, solved, tile_of))
    (pos,) = call(
        pos_kernel, "tile_places", [((NC,), jnp.int32)], [SMEM], (tile_now,), out_specs=[SMEM]
    )

    finished = []
    for step in range(STEPS - 1):
        if step == 1:
            routed, rhs_now = lax.optimization_barrier((routed, rhs))
            state0 = jnp.take(rhs_now, local_pivots, axis=1)
        back = swap_z(routed)
        extra = [outer] if step == 1 else []
        rows = ROWS * (1 + step)
        (message,) = call(
            lambda *refs: inverse_kernel(step, *refs),
            f"inverse_part_{step}",
            [((NZ, rows, TILE), BF)],
            [VMEM] * (2 + len(extra)),
            (back, start, *extra),
        )
        if step == 0:
            slot_known = jnp.where(my_block >= STEPS, solved_now[:, :TILE], 0.0)
            known = jnp.concatenate([slot_known, solved_now[:, TILE:]], axis=1).astype(BF)
            outer = lax.dot_general(
                known, lower_rows, (((1,), (2,)), ((), ())), preferred_element_type=F32
            )
            outer = outer.astype(BF).reshape(NZ, NY, rows_own, STEPS, TILE)
            outer = outer.transpose(1, 0, 2, 3, 4).reshape(NY, NZ * rows_own * STEPS, TILE)
            outer_sum = lax.dynamic_index_in_dim(outer, y, 0, False).astype(F32)
            for other in range(1, NY):
                theirs = lax.dynamic_index_in_dim(outer, y ^ other, 0, False)
                outer_sum = outer_sum + pass_y(theirs, other).astype(F32)
            outer = outer_sum.astype(BF).reshape(NZ, rows_own * STEPS, TILE)
            outer = jnp.pad(outer, ((0, 0), (0, ROWS - rows_own * STEPS), (0, 0)))
        outs = [((ROWS, TILE), BF), ((NP, NY * ROWS, TILE), BF)]
        if step == 1:
            outs.append(((ROWS, TILE), F32))
        value, message, *sums = call(
            lambda *refs: update_kernel(step, *refs),
            f"upper_update_{step}",
            outs,
            [VMEM] * (1 + NY),
            (swap_z(message), *near),
        )
        finished.append(value)
        outs = [((NZ * NY, ROWS, TILE), BF)]
        if step == 0:
            outs = [((NY, ROWS, TILE), F32), ((NZ, ROWS, TILE), BF)]
        found = call(
            lambda *refs: state_kernel(step, *refs),
            f"next_state_{step}",
            outs,
            [SMEM, VMEM, VMEM],
            (tile_of, swap_prow(message), tiles),
        )
        if step == 0:
            tiles, routed = found

    got = swap_z(found[0])
    order = jnp.arange(ROWS)
    pick_own = (
        (order[None, :] // rows_own == z) & (order[None, :] % rows_own == order[:, None] // PER)
    ).astype(BF)
    outer = sums[0][: rows_own * STEPS].reshape(rows_own, STEPS, TILE)
    outer = jnp.repeat(outer.transpose(1, 0, 2), PER, axis=1)
    last, message = last_call(pos, got, pick_own, outer[STEPS - 1], pack_all)
    finished.append(last)
    bases = [
        jnp.dot(pick_own, finished[step], preferred_element_type=F32) - outer[step]
        for step in range(STEPS - 1)
    ]

    message, pos_now = lax.optimization_barrier((message, pos))
    weights = fetch_call(1, pos_now, pack_all)
    stacked = jnp.concatenate(finished, axis=0)
    pair = jnp.stack([stacked, pass_y(stacked, 1)])
    back = swap_prow(message)
    last, message = lower_call(1, back, bases[1], weights, [])
    message, pair, pos_now = lax.optimization_barrier((message, pair, pos))
    weights = fetch_call(0, pos_now, pack_all)

    other = pass_y(pair, 2)
    every = [pair[0], pair[1], other[0], other[1]]
    every = by_place(every, y, NY).reshape(NY, STEPS, NZ, rows_own, TILE)
    every = every.transpose(1, 2, 0, 3, 4).reshape(STEPS, count, TILE)
    bulk = jnp.dot(
        jnp.concatenate(list(every), axis=1),
        upper_rows.reshape(STEPS * TILE, width),
        preferred_element_type=F32,
    )
    window_value = jnp.where(
        my_place == row, lax.dynamic_index_in_dim(every, jnp.minimum(my_block, STEPS - 1), 0, False), 0
    ).astype(F32)
    slot_bulk = jnp.where(my_block < STEPS, window_value, bulk[:, :TILE])
    bulk = jnp.concatenate([slot_bulk, bulk[:, TILE:]], axis=1).astype(BF)
    bulk = bulk.reshape(NP, count // NP * slots, TILE)

    back = swap_prow(message)
    middle, message = lower_call(0, back, bases[0], weights, [last])
    back = swap_prow(jnp.concatenate([message, bulk], axis=1))
    first = total(back[:, :ROWS]).astype(BF)

    window = jnp.concatenate([first, middle, last], axis=0)
    window = window.reshape(STEPS, rows_own, PER, TILE).transpose(0, 2, 1, 3)
    window = choose(window.reshape(STEPS * PER, rows_own, TILE), first_tiles)
    bulk = total(back[:, ROWS:]).astype(BF)
    window, bulk = lax.optimization_barrier((window, bulk))
    window = swap_pcol(window)
    pair = jnp.stack([bulk, pass_prow(bulk, 1)])
    pairs = [pair] + [pass_prow(pair, step) for step in range(2, NP, 2)]
    bulk = by_place([part[side] for part in pairs for side in range(2)], row, NP)
    bulk = bulk.reshape(count, width).astype(F32)
    slot_forward = jnp.where(my_block < STEPS, bulk[:, :TILE], state0[:, :TILE] - bulk[:, :TILE])
    forward = jnp.concatenate([slot_forward, state0[:, TILE:] - bulk[:, TILE:]], axis=1)
    forward, window = lax.optimization_barrier((forward, window))
    window = window.reshape(count, TILE).astype(F32)
    slot_solution = jnp.where(my_block < STEPS, window, solved[:, :TILE])
    backward = jnp.concatenate([slot_solution, solved[:, TILE:]], axis=1)
    return (forward, backward)


def solution(mesh):
    return jax.shard_map(
        body,
        mesh=mesh,
        in_specs=(
            P(None, "pcol"),
            P("pcol"),
            P(),
            P(None, "prow", "pcol"),
            P(None, "pcol", "prow"),
            P(None, "prow", "pcol"),
            P(None, "prow", "pcol"),
            P(None, "pcol"),
        ),
        out_specs=(P(None, "pcol"), P(None, "pcol")),
        check_vma=False,
    )
```

```python
import jax
import jax.numpy as jnp
from jax import lax
from jax.experimental import pallas as pl
from jax.experimental.pallas import tpu as pltpu
from jax.sharding import PartitionSpec as P

NB = 2048
TILE = 256
STEPS = 3
NY = 4
NZ = 8
NP = 8
NC = 32
PER = NB // TILE
PIECE = NB // NC
Y_GROUPS = [[z * NY + y for y in range(NY)] for z in range(NZ)]
Z_GROUPS = [[z * NY + y for z in range(NZ)] for y in range(NY)]
BF = jnp.bfloat16
F32 = jnp.float32
LOWER_AT = (STEPS - 1) * PIECE
PACK = LOWER_AT + (STEPS - 1) * TILE
UPPER_FIRST = 32
LOWER_LAST = UPPER_FIRST + PIECE
ROWS = 16
GRANT = 49 << 20
VMEM = pl.BlockSpec(memory_space=pltpu.VMEM)
SMEM = pl.BlockSpec(memory_space=pltpu.SMEM)
HBM = pl.BlockSpec(memory_space=pltpu.HBM)


def swap_y(x):
    return lax.all_to_all(x, "pcol", 0, 0, axis_index_groups=Y_GROUPS, tiled=True)


def pass_y(x, step):
    return lax.ppermute(x, "pcol", [(at, at ^ step) for at in range(NC)])


def pass_prow(x, step):
    return lax.ppermute(x, "prow", [(at, at ^ step) for at in range(NP)])


def by_place(parts, index, count):
    parts = jnp.stack(parts)
    return jnp.stack(
        [lax.dynamic_index_in_dim(parts, index ^ place, 0, False) for place in range(count)]
    )


def swap_z(x):
    return lax.all_to_all(x, "pcol", 0, 0, axis_index_groups=Z_GROUPS, tiled=True)


def swap_pcol(x):
    return lax.all_to_all(x, "pcol", 0, 0, tiled=True)


def swap_prow(x):
    return lax.all_to_all(x, "prow", 0, 0, tiled=True)


def to_all(x, count):
    return jnp.broadcast_to(x[None], (count,) + x.shape)


def total(x):
    return jnp.sum(x.astype(F32), axis=0)


def choose(values, index):
    where = (index[:, None] == jnp.arange(values.shape[0])[None, :]).astype(BF)
    flat = jnp.dot(where, values.reshape(values.shape[0], -1), preferred_element_type=F32)
    return flat.astype(BF).reshape((index.shape[0],) + values.shape[1:])


def dot_nt(a, b):
    return lax.dot_general(a, b, (((1,), (1,)), ((), ())), preferred_element_type=F32)


def dot_nn(a, b):
    return jnp.dot(a, b, preferred_element_type=F32)


def place_mask(place):
    return lax.broadcasted_iota(jnp.int32, (ROWS, TILE), 0) % PER == place


def lower_part(resid, inverse):
    full = dot_nt(resid, inverse[...].reshape(NB, TILE))
    part = full[:, :TILE]
    for place in range(1, PER):
        part = jnp.where(place_mask(place), full[:, place * TILE : (place + 1) * TILE], part)
    return part.astype(BF)


def call(kernel, name, outs, in_specs, args, scratch=(), out_specs=None, grant=None):
    return pl.pallas_call(
        kernel,
        out_shape=tuple(jax.ShapeDtypeStruct(shape, dtype) for shape, dtype in outs),
        in_specs=in_specs,
        out_specs=tuple(out_specs or [VMEM] * len(outs)),
        scratch_shapes=list(scratch),
        compiler_params=pltpu.CompilerParams(vmem_limit_bytes=grant or 8 << 20),
        name=name,
    )(*args)


def pos_kernel(tile_of, pos):
    stride = tile_of.shape[0] // NC

    def put(index, carry):
        pos[tile_of[index * stride]] = index
        return carry

    lax.fori_loop(0, NC, put, 0)


def plane():
    col = lax.axis_index("pcol")
    return col // NY, col % NY


def plane_tile(tile_of, z, other):
    return tile_of[(z * NY + other) * (tile_of.shape[0] // NC)]


def first_kernel(tile_of, got, inverses, tiles, message):
    z, y = plane()
    for index in range(NZ):
        message[index, pl.ds(0, ROWS), :] = jnp.zeros((ROWS, TILE), BF)
        message[index, pl.ds(ROWS, (STEPS - 1) * PIECE), :] = inverses[...]
    for step in range(NY):
        other = y ^ step
        value = got[other, pl.ds(0, ROWS), :].astype(F32)
        value = value + got[other, pl.ds(ROWS, ROWS), :].astype(F32)
        tiles[step] = value
        tile = plane_tile(tile_of, z, other)

        @pl.when(tile // PER == 0)
        def _():
            message[tile % PER, pl.ds(0, ROWS), :] = value.astype(BF)


def stacked_rows(got, at):
    return jnp.concatenate([got[other, pl.ds(at, PIECE), :] for other in range(NY)], axis=0)


def inverse_kernel(tile_of, back, got, message, picked):
    mine = jnp.sum(back[:, pl.ds(0, ROWS), :].astype(F32), axis=0).astype(BF)
    part = dot_nn(mine, stacked_rows(got, UPPER_FIRST)).astype(BF)
    for index in range(NZ):
        message[index] = part
    z, _ = plane()
    for other in range(NY):
        tile = plane_tile(tile_of, z, other)
        near = back[tile % PER, pl.ds(ROWS, PIECE), :]
        far = back[tile % PER, pl.ds(ROWS + PIECE, PIECE), :]
        one = (tile // PER == 1).astype(BF)
        two = (tile // PER == 2).astype(BF)
        picked[other] = near * one + far * two


def update_kernel(step, back, own, near_1, near_2, near_3, solved_out, message, *outer):
    sums = jnp.sum(back[...].astype(F32), axis=0)
    value = sums[:ROWS].astype(BF)
    solved_out[...] = value
    if outer:
        outer[0][...] = sums[ROWS:]
    for index, near in enumerate((own, near_1, near_2, near_3)):
        update = dot_nn(value, near[pl.ds(step * TILE, TILE), :]).astype(BF)
        for other in range(NP):
            message[other, pl.ds(index * ROWS, ROWS), :] = update


def state_kernel(step, tile_of, back, tiles, parts, *rest):
    z, y = plane()
    sums = jnp.sum(back[...].astype(F32), axis=0)
    message = rest[-1]
    part = jnp.zeros((ROWS, TILE), F32)
    for index in range(NY):
        other = y ^ index
        tile = plane_tile(tile_of, z, other)
        keep = (tile // PER > step).astype(F32)
        value = tiles[index] - keep * sums[index * ROWS : (index + 1) * ROWS]
        if step == 0:
            rest[2][index] = value
        block = (value * (tile // PER == step + 1).astype(F32)).astype(BF)
        weights = jnp.concatenate([parts[sub ^ y, other] for sub in range(NY)], axis=0)
        part = part + dot_nn(block, weights)
    part = part.astype(BF)
    for index in range(NZ):
        message[index, pl.ds(0, ROWS), :] = part
        if step == 0:
            message[index, pl.ds(ROWS, ROWS), :] = rest[0][...]
            message[index, pl.ds(2 * ROWS, ROWS), :] = rest[1][index]


def last_kernel(back, outer, got, solved_out, message):
    value = jnp.sum(back[...].astype(F32), axis=0).astype(BF)
    solved_out[...] = value
    resid = (value.astype(F32) - outer[...]).astype(BF)
    part = dot_nt(resid, stacked_rows(got, LOWER_LAST)).astype(BF)
    for index in range(NP):
        message[index] = part


def share_kernel(back, message):
    value = jnp.sum(back[...].astype(F32), axis=0).astype(BF)
    for index in range(NZ):
        message[index] = value


def fetch_kernel(step, pos, pack, tiles, inverse, sems):
    copies = [
        pltpu.make_async_copy(
            pack.at[pos[(step + 1 + at) * PER + place], pl.ds(LOWER_AT + step * TILE, TILE), :],
            tiles.at[at, :, pl.ds(place * TILE, TILE)],
            sems.at[at * PER + place],
        )
        for at in range(STEPS - 1 - step)
        for place in range(PER)
    ]
    copies.append(
        pltpu.make_async_copy(
            pack.at[:, pl.ds(step * PIECE, PIECE), :], inverse, sems.at[len(copies)]
        )
    )
    for copy in copies:
        copy.start()
    for copy in copies:
        copy.wait()


def fetch_call(step, pos, pack):
    later = STEPS - 1 - step
    return call(
        lambda *refs: fetch_kernel(step, *refs),
        f"fetch_block_{step}",
        [((later, TILE, NB), BF), ((NC, PIECE, TILE), BF)],
        [SMEM, HBM],
        (pos, pack),
        [pltpu.SemaphoreType.DMA((later * PER + 1,))],
        grant=GRANT,
    )


def lower_kernel(step, back, base, tiles, inverse, *rest):
    known = rest[:-2]
    value_out, message_out = rest[-2:]
    if step == STEPS - 2:
        pick_own = known[0][...]
        value = jnp.zeros((ROWS, TILE), F32)
        for place in range(PER):
            value = jnp.where(place_mask(place), dot_nn(pick_own, back[place]), value)
        value = value.astype(BF)
    else:
        value = jnp.sum(back[...].astype(F32), axis=0).astype(BF)
    value_out[...] = value
    sums = jnp.zeros((ROWS, TILE), F32)
    for at in range(STEPS - 1 - step):
        solved = value if at == 0 else known[at - 1][...]
        wide = jnp.concatenate(
            [jnp.where(place_mask(place), solved, jnp.zeros_like(solved)) for place in range(PER)],
            axis=1,
        )
        sums = sums + dot_nt(wide, tiles[at])
    sums = jnp.sum(sums.reshape(ROWS // PER, PER, TILE), axis=1, keepdims=True)
    sums = jnp.broadcast_to(sums, (ROWS // PER, PER, TILE)).reshape(ROWS, TILE)
    part = lower_part((base[...] - sums).astype(BF), inverse)
    for index in range(NP):
        message_out[index] = part


def lower_call(step, back, base, weights, known):
    return call(
        lambda *refs: lower_kernel(step, *refs),
        f"lower_block_{step}",
        [((ROWS, TILE), BF), ((NP, ROWS, TILE), BF)],
        [VMEM] * (4 + len(known)),
        (back, base, *weights, *known),
        grant=16 << 20,
    )


def body(rhs, pivots, tile_of, upper_rows, upper_inv, lower_rows, lower_inv, solved):
    col = lax.axis_index("pcol")
    row = lax.axis_index("prow")
    z = col // NY
    y = col % NY
    count, width = rhs.shape
    slots = width // TILE
    rows_z = count // NY
    rows_own = count // NC
    first_tiles = tile_of.reshape(NC, slots)[:, 0]
    my_tile = first_tiles[col]
    my_block = my_tile // PER
    my_place = my_tile % PER

    lower_turned = jnp.swapaxes(lower_inv, 1, 2)
    pack = jnp.concatenate(
        [
            lower_turned[: STEPS - 1].reshape(LOWER_AT, TILE),
            lower_rows[: STEPS - 1, :, :TILE].reshape(PACK - LOWER_AT, TILE),
        ],
        axis=0,
    )
    pack_all = lax.all_gather(pack, "pcol", axis=0)

    local_pivots = pivots - col * width
    own = jnp.take(rhs[:, :TILE], local_pivots[:TILE], axis=1)
    own = own.reshape(NZ, NY, rows_own, TILE).transpose(1, 0, 2, 3).reshape(NY, rows_z, TILE)
    own_high = own.astype(BF)
    own_low = (own - own_high.astype(F32)).astype(BF)
    both = jnp.concatenate([upper_inv[0], lower_turned[STEPS - 1]], axis=0)
    start = swap_y(jnp.concatenate([own_high, own_low, to_all(both, NY)], axis=1))
    tiles, message = call(
        first_kernel,
        "first_state",
        [((NY, ROWS, TILE), F32), ((NZ, ROWS + (STEPS - 1) * PIECE, TILE), BF)],
        [SMEM, VMEM, VMEM],
        (tile_of, start, upper_inv[1:].reshape((STEPS - 1) * PIECE, TILE)),
    )
    upper_pack = upper_rows[: STEPS - 1, :, :TILE].reshape((STEPS - 1) * TILE, TILE)
    near = [upper_pack] + [pass_y(upper_pack, step) for step in range(1, NY)]
    message, solved_now, tile_now = lax.optimization_barrier((message, solved, tile_of))
    (pos,) = call(
        pos_kernel, "tile_places", [((NC,), jnp.int32)], [SMEM], (tile_now,), out_specs=[SMEM]
    )
    message, picked = call(
        inverse_kernel,
        "inverse_part_0",
        [((NZ, ROWS, TILE), BF), ((NY, PIECE, TILE), BF)],
        [SMEM, VMEM, VMEM],
        (tile_of, swap_z(message), start),
    )
    parts = jnp.stack([picked] + [pass_y(picked, step) for step in range(1, NY)])

    slot_known = jnp.where(my_block >= STEPS, solved_now[:, :TILE], 0.0)
    known = jnp.concatenate([slot_known, solved_now[:, TILE:]], axis=1).astype(BF)
    outer = lax.dot_general(
        known, lower_rows, (((1,), (2,)), ((), ())), preferred_element_type=F32
    )
    outer = outer.astype(BF).reshape(NZ, NY, rows_own, STEPS, TILE)
    outer = outer.transpose(1, 0, 2, 3, 4).reshape(NY, NZ * rows_own * STEPS, TILE)
    outer_sum = lax.dynamic_index_in_dim(outer, y, 0, False).astype(F32)
    for other in range(1, NY):
        theirs = lax.dynamic_index_in_dim(outer, y ^ other, 0, False)
        outer_sum = outer_sum + pass_y(theirs, other).astype(F32)
    outer = outer_sum.astype(BF).reshape(NZ, rows_own, STEPS, TILE)
    outer_last = outer[:, :, STEPS - 1].reshape(ROWS, TILE)
    outer_rest = outer[:, :, : STEPS - 1].reshape(NZ, rows_own * (STEPS - 1), TILE)
    outer_rest = jnp.pad(outer_rest, ((0, 0), (0, ROWS - rows_own * (STEPS - 1)), (0, 0)))

    finished = []
    for step in range(STEPS - 1):
        outs = [((ROWS, TILE), BF), ((NP, NY * ROWS, TILE), BF)]
        if step == 1:
            outs.append(((2 * ROWS, TILE), F32))
        value, message, *sums = call(
            lambda *refs: update_kernel(step, *refs),
            f"upper_update_{step}",
            outs,
            [VMEM] * (1 + NY),
            (swap_z(message), *near),
        )
        finished.append(value)
        back = swap_prow(message)
        if step == 0:
            tiles, message = call(
                lambda *refs: state_kernel(0, *refs),
                "next_state_0",
                [((NY, ROWS, TILE), F32), ((NZ, 3 * ROWS, TILE), BF)],
                [SMEM] + [VMEM] * 5,
                (tile_of, back, tiles, parts, outer_last, outer_rest),
            )
        else:
            (message,) = call(
                lambda *refs: state_kernel(1, *refs),
                "next_state_1",
                [((NZ, ROWS, TILE), BF)],
                [SMEM] + [VMEM] * 3,
                (tile_of, back, tiles, parts),
            )

    order = jnp.arange(ROWS)
    pick_own = (
        (order[None, :] // rows_own == z) & (order[None, :] % rows_own == order[:, None] // PER)
    ).astype(BF)
    outer = sums[0][ROWS : ROWS + rows_own * (STEPS - 1)].reshape(rows_own, STEPS - 1, TILE)
    outer = jnp.repeat(outer.transpose(1, 0, 2), PER, axis=1)
    last, message = call(
        last_kernel,
        "last_block",
        [((ROWS, TILE), BF), ((NP, ROWS, TILE), BF)],
        [VMEM] * 3,
        (swap_z(message), sums[0][:ROWS], start),
    )
    finished.append(last)
    bases = [
        jnp.dot(pick_own, finished[step], preferred_element_type=F32) - outer[step]
        for step in range(STEPS - 1)
    ]
    stacked = jnp.concatenate(finished, axis=0)
    pair = jnp.stack([stacked, pass_y(stacked, 1)])
    (message,) = call(
        share_kernel, "share_last", [((NZ, ROWS, TILE), BF)], [VMEM], (swap_prow(message),)
    )
    message, pair, pos_now = lax.optimization_barrier((message, pair, pos))
    weights = fetch_call(1, pos_now, pack_all)
    last, message = lower_call(1, swap_z(message), bases[1], weights, [pick_own])

    other = pass_y(pair, 2)
    every = [pair[0], pair[1], other[0], other[1]]
    every = by_place(every, y, NY).reshape(NY, STEPS, NZ, rows_own, TILE)
    every = every.transpose(1, 2, 0, 3, 4).reshape(STEPS, count, TILE)
    bulk = jnp.dot(
        jnp.concatenate(list(every), axis=1),
        upper_rows.reshape(STEPS * TILE, width),
        preferred_element_type=F32,
    )
    window_value = jnp.where(
        my_place == row, lax.dynamic_index_in_dim(every, jnp.minimum(my_block, STEPS - 1), 0, False), 0
    ).astype(F32)
    slot_bulk = jnp.where(my_block < STEPS, window_value, bulk[:, :TILE])
    bulk = jnp.concatenate([slot_bulk, bulk[:, TILE:]], axis=1).astype(BF)
    bulk = bulk.reshape(NP, count // NP * slots, TILE)

    message, pos_now = lax.optimization_barrier((message, pos))
    weights = fetch_call(0, pos_now, pack_all)
    back = swap_prow(jnp.concatenate([message, bulk], axis=1))
    middle, message = lower_call(0, back[:, :ROWS], bases[0], weights, [last])
    message, rhs_now = lax.optimization_barrier((message, rhs))
    state0 = jnp.take(rhs_now, local_pivots, axis=1)
    first = total(swap_prow(message)).astype(BF)

    window = jnp.concatenate([first, middle, last], axis=0)
    window = window.reshape(STEPS, rows_own, PER, TILE).transpose(0, 2, 1, 3)
    window = choose(window.reshape(STEPS * PER, rows_own, TILE), first_tiles)
    bulk = total(back[:, ROWS:]).astype(BF)
    window, bulk = lax.optimization_barrier((window, bulk))
    window = swap_pcol(window)
    pair = jnp.stack([bulk, pass_prow(bulk, 1)])
    pairs = [pair] + [pass_prow(pair, step) for step in range(2, NP, 2)]
    bulk = by_place([part[side] for part in pairs for side in range(2)], row, NP)
    bulk = bulk.reshape(count, width).astype(F32)
    slot_forward = jnp.where(my_block < STEPS, bulk[:, :TILE], state0[:, :TILE] - bulk[:, :TILE])
    forward = jnp.concatenate([slot_forward, state0[:, TILE:] - bulk[:, TILE:]], axis=1)
    forward, window = lax.optimization_barrier((forward, window))
    window = window.reshape(count, TILE).astype(F32)
    slot_solution = jnp.where(my_block < STEPS, window, solved[:, :TILE])
    backward = jnp.concatenate([slot_solution, solved[:, TILE:]], axis=1)
    return (forward, backward)


def solution(mesh):
    return jax.shard_map(
        body,
        mesh=mesh,
        in_specs=(
            P(None, "pcol"),
            P("pcol"),
            P(),
            P(None, "prow", "pcol"),
            P(None, "pcol", "prow"),
            P(None, "prow", "pcol"),
            P(None, "prow", "pcol"),
            P(None, "pcol"),
        ),
        out_specs=(P(None, "pcol"), P(None, "pcol")),
        check_vma=False,
    )
```

```python
import jax
import jax.numpy as jnp
from jax import lax
from jax.experimental import pallas as pl
from jax.experimental.pallas import tpu as pltpu
from jax.sharding import PartitionSpec as P

NB = 2048
TILE = 256
STEPS = 3
NY = 4
NZ = 8
NP = 8
NC = 32
PER = NB // TILE
PIECE = NB // NC
Y_GROUPS = [[z * NY + y for y in range(NY)] for z in range(NZ)]
Z_GROUPS = [[z * NY + y for z in range(NZ)] for y in range(NY)]
BF = jnp.bfloat16
F32 = jnp.float32
LOWER_AT = (STEPS - 1) * PIECE
PACK = LOWER_AT + (STEPS - 1) * TILE
UPPER_FIRST = 32
LOWER_LAST = UPPER_FIRST + PIECE
ROWS = 16
GRANT = 49 << 20
VMEM = pl.BlockSpec(memory_space=pltpu.VMEM)
SMEM = pl.BlockSpec(memory_space=pltpu.SMEM)
HBM = pl.BlockSpec(memory_space=pltpu.HBM)


def swap_y(x):
    return lax.all_to_all(x, "pcol", 0, 0, axis_index_groups=Y_GROUPS, tiled=True)


def pass_y(x, step):
    return lax.ppermute(x, "pcol", [(at, at ^ step) for at in range(NC)])


def pass_prow(x, step):
    return lax.ppermute(x, "prow", [(at, at ^ step) for at in range(NP)])


def by_place(parts, index, count):
    parts = jnp.stack(parts)
    return jnp.stack(
        [lax.dynamic_index_in_dim(parts, index ^ place, 0, False) for place in range(count)]
    )


def swap_z(x):
    return lax.all_to_all(x, "pcol", 0, 0, axis_index_groups=Z_GROUPS, tiled=True)


def swap_pcol(x):
    return lax.all_to_all(x, "pcol", 0, 0, tiled=True)


def swap_prow(x):
    return lax.all_to_all(x, "prow", 0, 0, tiled=True)


def to_all(x, count):
    return jnp.broadcast_to(x[None], (count,) + x.shape)


def total(x):
    return jnp.sum(x.astype(F32), axis=0)


def choose(values, index):
    where = (index[:, None] == jnp.arange(values.shape[0])[None, :]).astype(BF)
    flat = jnp.dot(where, values.reshape(values.shape[0], -1), preferred_element_type=F32)
    return flat.astype(BF).reshape((index.shape[0],) + values.shape[1:])


def dot_nt(a, b):
    return lax.dot_general(a, b, (((1,), (1,)), ((), ())), preferred_element_type=F32)


def dot_nn(a, b):
    return jnp.dot(a, b, preferred_element_type=F32)


def place_mask(place):
    return lax.broadcasted_iota(jnp.int32, (ROWS, TILE), 0) % PER == place


def lower_part(resid, inverse):
    full = dot_nt(resid, inverse[...].reshape(NB, TILE))
    part = full[:, :TILE]
    for place in range(1, PER):
        part = jnp.where(place_mask(place), full[:, place * TILE : (place + 1) * TILE], part)
    return part.astype(BF)


def call(kernel, name, outs, in_specs, args, scratch=(), out_specs=None, grant=None):
    return pl.pallas_call(
        kernel,
        out_shape=tuple(jax.ShapeDtypeStruct(shape, dtype) for shape, dtype in outs),
        in_specs=in_specs,
        out_specs=tuple(out_specs or [VMEM] * len(outs)),
        scratch_shapes=list(scratch),
        compiler_params=pltpu.CompilerParams(vmem_limit_bytes=grant or 8 << 20),
        name=name,
    )(*args)


def pos_kernel(tile_of, pos):
    stride = tile_of.shape[0] // NC

    def put(index, carry):
        pos[tile_of[index * stride]] = index
        return carry

    lax.fori_loop(0, NC, put, 0)


def plane():
    col = lax.axis_index("pcol")
    return col // NY, col % NY


def plane_tile(tile_of, z, other):
    return tile_of[(z * NY + other) * (tile_of.shape[0] // NC)]


def first_kernel(tile_of, got, inverses, tiles, message):
    z, y = plane()
    for index in range(NZ):
        message[index, pl.ds(0, ROWS), :] = jnp.zeros((ROWS, TILE), BF)
        message[index, pl.ds(ROWS, (STEPS - 1) * PIECE), :] = inverses[...]
    for step in range(NY):
        other = y ^ step
        value = got[other, pl.ds(0, ROWS), :].astype(F32)
        value = value + got[other, pl.ds(ROWS, ROWS), :].astype(F32)
        tiles[step] = value
        tile = plane_tile(tile_of, z, other)

        @pl.when(tile // PER == 0)
        def _():
            message[tile % PER, pl.ds(0, ROWS), :] = value.astype(BF)


def stacked_rows(got, at):
    return jnp.concatenate([got[other, pl.ds(at, PIECE), :] for other in range(NY)], axis=0)


def inverse_kernel(tile_of, back, got, message, picked):
    mine = jnp.sum(back[:, pl.ds(0, ROWS), :].astype(F32), axis=0).astype(BF)
    part = dot_nn(mine, stacked_rows(got, UPPER_FIRST)).astype(BF)
    for index in range(NZ):
        message[index] = part
    z, _ = plane()
    for other in range(NY):
        tile = plane_tile(tile_of, z, other)
        near = back[tile % PER, pl.ds(ROWS, PIECE), :]
        far = back[tile % PER, pl.ds(ROWS + PIECE, PIECE), :]
        one = (tile // PER == 1).astype(BF)
        two = (tile // PER == 2).astype(BF)
        picked[other] = near * one + far * two


def update_kernel(step, back, own, near_1, near_2, near_3, solved_out, message, *outer):
    sums = jnp.sum(back[...].astype(F32), axis=0)
    value = sums[:ROWS].astype(BF)
    solved_out[...] = value
    if outer:
        outer[0][...] = sums[ROWS:]
    for index, near in enumerate((own, near_1, near_2, near_3)):
        update = dot_nn(value, near[pl.ds(step * TILE, TILE), :]).astype(BF)
        for other in range(NP):
            message[other, pl.ds(index * ROWS, ROWS), :] = update


def state_kernel(step, tile_of, back, tiles, parts, *rest):
    z, y = plane()
    sums = jnp.sum(back[...].astype(F32), axis=0)
    message = rest[-1]
    part = jnp.zeros((ROWS, TILE), F32)
    for index in range(NY):
        other = y ^ index
        tile = plane_tile(tile_of, z, other)
        keep = (tile // PER > step).astype(F32)
        value = tiles[index] - keep * sums[index * ROWS : (index + 1) * ROWS]
        if step == 0:
            rest[2][index] = value
        block = (value * (tile // PER == step + 1).astype(F32)).astype(BF)
        weights = jnp.concatenate([parts[sub ^ y, other] for sub in range(NY)], axis=0)
        part = part + dot_nn(block, weights)
    part = part.astype(BF)
    for index in range(NZ):
        message[index, pl.ds(0, ROWS), :] = part
        if step == 0:
            message[index, pl.ds(ROWS, ROWS), :] = rest[0][...]
            message[index, pl.ds(2 * ROWS, ROWS), :] = rest[1][index]


def last_kernel(back, outer, got, solved_out, message):
    value = jnp.sum(back[...].astype(F32), axis=0).astype(BF)
    solved_out[...] = value
    resid = (value.astype(F32) - outer[...]).astype(BF)
    part = dot_nt(resid, stacked_rows(got, LOWER_LAST)).astype(BF)
    for index in range(NP):
        message[index] = part


def share_kernel(back, message):
    value = jnp.sum(back[...].astype(F32), axis=0).astype(BF)
    for index in range(NZ):
        message[index] = value


def fetch_kernel(step, pos, pack, tiles, inverse, sems):
    copies = [
        pltpu.make_async_copy(
            pack.at[pos[(step + 1 + at) * PER + place], pl.ds(LOWER_AT + step * TILE, TILE), :],
            tiles.at[at, :, pl.ds(place * TILE, TILE)],
            sems.at[at * PER + place],
        )
        for at in range(STEPS - 1 - step)
        for place in range(PER)
    ]
    copies.append(
        pltpu.make_async_copy(
            pack.at[:, pl.ds(step * PIECE, PIECE), :], inverse, sems.at[len(copies)]
        )
    )
    for copy in copies:
        copy.start()
    for copy in copies:
        copy.wait()


def fetch_call(step, pos, pack):
    later = STEPS - 1 - step
    return call(
        lambda *refs: fetch_kernel(step, *refs),
        f"fetch_block_{step}",
        [((later, TILE, NB), BF), ((NC, PIECE, TILE), BF)],
        [SMEM, HBM],
        (pos, pack),
        [pltpu.SemaphoreType.DMA((later * PER + 1,))],
        grant=GRANT,
    )


def lower_kernel(step, back, base, tiles, inverse, *rest):
    outs = 2 if step == STEPS - 2 else 3
    known = rest[:-outs]
    value_out, message_out = rest[-outs : len(rest) - outs + 2]
    if step == STEPS - 2:
        pick_own = known[0][...]
        value = jnp.zeros((ROWS, TILE), F32)
        for place in range(PER):
            value = jnp.where(place_mask(place), dot_nn(pick_own, back[place]), value)
        value = value.astype(BF)
    else:
        value = jnp.sum(back[:, pl.ds(0, ROWS), :].astype(F32), axis=0).astype(BF)
        bulk = jnp.sum(back[:, pl.ds(ROWS, back.shape[1] - ROWS), :].astype(F32), axis=0)
        rest[-1][...] = bulk.astype(BF)
    value_out[...] = value
    sums = jnp.zeros((ROWS, TILE), F32)
    for at in range(STEPS - 1 - step):
        solved = value if at == 0 else known[at - 1][...]
        wide = jnp.concatenate(
            [jnp.where(place_mask(place), solved, jnp.zeros_like(solved)) for place in range(PER)],
            axis=1,
        )
        sums = sums + dot_nt(wide, tiles[at])
    sums = jnp.sum(sums.reshape(ROWS // PER, PER, TILE), axis=1, keepdims=True)
    sums = jnp.broadcast_to(sums, (ROWS // PER, PER, TILE)).reshape(ROWS, TILE)
    part = lower_part((base[...] - sums).astype(BF), inverse)
    for index in range(NP):
        message_out[index, pl.ds(0, ROWS), :] = part
        if step == STEPS - 2:
            message_out[index, pl.ds(ROWS, known[1].shape[1]), :] = known[1][index]


def lower_call(step, back, base, weights, known):
    outs = [((ROWS, TILE), BF), ((NP, ROWS, TILE), BF)]
    if step == STEPS - 2:
        outs[1] = ((NP, ROWS + known[1].shape[1], TILE), BF)
    else:
        outs.append(((back.shape[1] - ROWS, TILE), BF))
    return call(
        lambda *refs: lower_kernel(step, *refs),
        f"lower_block_{step}",
        outs,
        [VMEM] * (4 + len(known)),
        (back, base, *weights, *known),
        grant=16 << 20,
    )


def body(rhs, pivots, tile_of, upper_rows, upper_inv, lower_rows, lower_inv, solved):
    col = lax.axis_index("pcol")
    row = lax.axis_index("prow")
    z = col // NY
    y = col % NY
    count, width = rhs.shape
    slots = width // TILE
    rows_z = count // NY
    rows_own = count // NC
    first_tiles = tile_of.reshape(NC, slots)[:, 0]
    my_tile = first_tiles[col]
    my_block = my_tile // PER
    my_place = my_tile % PER

    lower_turned = jnp.swapaxes(lower_inv, 1, 2)
    pack = jnp.concatenate(
        [
            lower_turned[: STEPS - 1].reshape(LOWER_AT, TILE),
            lower_rows[: STEPS - 1, :, :TILE].reshape(PACK - LOWER_AT, TILE),
        ],
        axis=0,
    )
    pack_all = lax.all_gather(pack, "pcol", axis=0)

    local_pivots = pivots - col * width
    own = jnp.take(rhs[:, :TILE], local_pivots[:TILE], axis=1)
    own = own.reshape(NZ, NY, rows_own, TILE).transpose(1, 0, 2, 3).reshape(NY, rows_z, TILE)
    own_high = own.astype(BF)
    own_low = (own - own_high.astype(F32)).astype(BF)
    both = jnp.concatenate([upper_inv[0], lower_turned[STEPS - 1]], axis=0)
    start = swap_y(jnp.concatenate([own_high, own_low, to_all(both, NY)], axis=1))
    tiles, message = call(
        first_kernel,
        "first_state",
        [((NY, ROWS, TILE), F32), ((NZ, ROWS + (STEPS - 1) * PIECE, TILE), BF)],
        [SMEM, VMEM, VMEM],
        (tile_of, start, upper_inv[1:].reshape((STEPS - 1) * PIECE, TILE)),
    )
    upper_pack = upper_rows[: STEPS - 1, :, :TILE].reshape((STEPS - 1) * TILE, TILE)
    near = [upper_pack] + [pass_y(upper_pack, step) for step in range(1, NY)]
    message, solved_now, tile_now = lax.optimization_barrier((message, solved, tile_of))
    (pos,) = call(
        pos_kernel, "tile_places", [((NC,), jnp.int32)], [SMEM], (tile_now,), out_specs=[SMEM]
    )
    message, picked = call(
        inverse_kernel,
        "inverse_part_0",
        [((NZ, ROWS, TILE), BF), ((NY, PIECE, TILE), BF)],
        [SMEM, VMEM, VMEM],
        (tile_of, swap_z(message), start),
    )
    parts = jnp.stack([picked] + [pass_y(picked, step) for step in range(1, NY)])

    slot_known = jnp.where(my_block >= STEPS, solved_now[:, :TILE], 0.0)
    known = jnp.concatenate([slot_known, solved_now[:, TILE:]], axis=1).astype(BF)
    outer = lax.dot_general(
        known, lower_rows, (((1,), (2,)), ((), ())), preferred_element_type=F32
    )
    outer = outer.astype(BF).reshape(NZ, NY, rows_own, STEPS, TILE)
    outer = outer.transpose(1, 0, 2, 3, 4).reshape(NY, NZ * rows_own * STEPS, TILE)
    outer_sum = lax.dynamic_index_in_dim(outer, y, 0, False).astype(F32)
    for other in range(1, NY):
        theirs = lax.dynamic_index_in_dim(outer, y ^ other, 0, False)
        outer_sum = outer_sum + pass_y(theirs, other).astype(F32)
    outer = outer_sum.astype(BF).reshape(NZ, rows_own, STEPS, TILE)
    outer_last = outer[:, :, STEPS - 1].reshape(ROWS, TILE)
    outer_rest = outer[:, :, : STEPS - 1].reshape(NZ, rows_own * (STEPS - 1), TILE)
    outer_rest = jnp.pad(outer_rest, ((0, 0), (0, ROWS - rows_own * (STEPS - 1)), (0, 0)))

    finished = []
    for step in range(STEPS - 1):
        outs = [((ROWS, TILE), BF), ((NP, NY * ROWS, TILE), BF)]
        if step == 1:
            outs.append(((2 * ROWS, TILE), F32))
        value, message, *sums = call(
            lambda *refs: update_kernel(step, *refs),
            f"upper_update_{step}",
            outs,
            [VMEM] * (1 + NY),
            (swap_z(message), *near),
        )
        finished.append(value)
        back = swap_prow(message)
        if step == 0:
            tiles, message = call(
                lambda *refs: state_kernel(0, *refs),
                "next_state_0",
                [((NY, ROWS, TILE), F32), ((NZ, 3 * ROWS, TILE), BF)],
                [SMEM] + [VMEM] * 5,
                (tile_of, back, tiles, parts, outer_last, outer_rest),
            )
            message, rhs_now = lax.optimization_barrier((message, rhs))
            state0 = jnp.take(rhs_now, local_pivots, axis=1)
        else:
            (message,) = call(
                lambda *refs: state_kernel(1, *refs),
                "next_state_1",
                [((NZ, ROWS, TILE), BF)],
                [SMEM] + [VMEM] * 3,
                (tile_of, back, tiles, parts),
            )
            message, state0 = lax.optimization_barrier((message, state0))

    order = jnp.arange(ROWS)
    pick_own = (
        (order[None, :] // rows_own == z) & (order[None, :] % rows_own == order[:, None] // PER)
    ).astype(BF)
    outer = sums[0][ROWS : ROWS + rows_own * (STEPS - 1)].reshape(rows_own, STEPS - 1, TILE)
    outer = jnp.repeat(outer.transpose(1, 0, 2), PER, axis=1)
    last, message = call(
        last_kernel,
        "last_block",
        [((ROWS, TILE), BF), ((NP, ROWS, TILE), BF)],
        [VMEM] * 3,
        (swap_z(message), sums[0][:ROWS], start),
    )
    finished.append(last)
    bases = [
        jnp.dot(pick_own, finished[step], preferred_element_type=F32) - outer[step]
        for step in range(STEPS - 1)
    ]
    stacked = jnp.concatenate(finished, axis=0)
    pair = jnp.stack([stacked, pass_y(stacked, 1)])
    (message,) = call(
        share_kernel, "share_last", [((NZ, ROWS, TILE), BF)], [VMEM], (swap_prow(message),)
    )
    message, pair, pos_now = lax.optimization_barrier((message, pair, pos))
    weights = fetch_call(1, pos_now, pack_all)
    shared = swap_z(message)

    other = pass_y(pair, 2)
    every = [pair[0], pair[1], other[0], other[1]]
    every = by_place(every, y, NY).reshape(NY, STEPS, NZ, rows_own, TILE)
    every = every.transpose(1, 2, 0, 3, 4).reshape(STEPS, count, TILE)
    bulk = jnp.dot(
        jnp.concatenate(list(every), axis=1),
        upper_rows.reshape(STEPS * TILE, width),
        preferred_element_type=F32,
    )
    window_value = jnp.where(
        my_place == row, lax.dynamic_index_in_dim(every, jnp.minimum(my_block, STEPS - 1), 0, False), 0
    ).astype(F32)
    slot_bulk = jnp.where(my_block < STEPS, window_value, bulk[:, :TILE])
    bulk = jnp.concatenate([slot_bulk, bulk[:, TILE:]], axis=1).astype(BF)
    bulk = bulk.reshape(NP, count // NP * slots, TILE)

    last, message = lower_call(1, shared, bases[1], weights, [pick_own, bulk])
    message, pos_now = lax.optimization_barrier((message, pos))
    weights = fetch_call(0, pos_now, pack_all)
    back = swap_prow(message)
    middle, message, bulk = lower_call(0, back, bases[0], weights, [last])
    first = total(swap_prow(message)).astype(BF)

    window = jnp.concatenate([first, middle, last], axis=0)
    window = window.reshape(STEPS, rows_own, PER, TILE).transpose(0, 2, 1, 3)
    window = choose(window.reshape(STEPS * PER, rows_own, TILE), first_tiles)
    window = swap_pcol(window)
    pair = jnp.stack([bulk, pass_prow(bulk, 1)])
    pairs = [pair] + [pass_prow(pair, step) for step in range(2, NP, 2)]
    bulk = by_place([part[side] for part in pairs for side in range(2)], row, NP)
    bulk = bulk.reshape(count, width).astype(F32)
    slot_forward = jnp.where(my_block < STEPS, bulk[:, :TILE], state0[:, :TILE] - bulk[:, :TILE])
    forward = jnp.concatenate([slot_forward, state0[:, TILE:] - bulk[:, TILE:]], axis=1)
    forward, window = lax.optimization_barrier((forward, window))
    window = window.reshape(count, TILE).astype(F32)
    slot_solution = jnp.where(my_block < STEPS, window, solved[:, :TILE])
    backward = jnp.concatenate([slot_solution, solved[:, TILE:]], axis=1)
    return (forward, backward)


def solution(mesh):
    return jax.shard_map(
        body,
        mesh=mesh,
        in_specs=(
            P(None, "pcol"),
            P("pcol"),
            P(),
            P(None, "prow", "pcol"),
            P(None, "pcol", "prow"),
            P(None, "prow", "pcol"),
            P(None, "prow", "pcol"),
            P(None, "pcol"),
        ),
        out_specs=(P(None, "pcol"), P(None, "pcol")),
        check_vma=False,
    )
```

```python
import jax
import jax.numpy as jnp
from jax import lax
from jax.experimental import pallas as pl
from jax.experimental.pallas import tpu as pltpu
from jax.sharding import PartitionSpec as P

NB = 2048
TILE = 256
STEPS = 3
NY = 4
NZ = 8
NP = 8
NC = 32
PER = NB // TILE
PIECE = NB // NC
Y_GROUPS = [[z * NY + y for y in range(NY)] for z in range(NZ)]
Z_GROUPS = [[z * NY + y for z in range(NZ)] for y in range(NY)]
BF = jnp.bfloat16
F32 = jnp.float32
LOWER_AT = (STEPS - 1) * PIECE
PACK = LOWER_AT + (STEPS - 1) * TILE
UPPER_FIRST = 32
LOWER_LAST = UPPER_FIRST + PIECE
ROWS = 16
GRANT = 49 << 20
VMEM = pl.BlockSpec(memory_space=pltpu.VMEM)
SMEM = pl.BlockSpec(memory_space=pltpu.SMEM)
HBM = pl.BlockSpec(memory_space=pltpu.HBM)


def swap_y(x):
    return lax.all_to_all(x, "pcol", 0, 0, axis_index_groups=Y_GROUPS, tiled=True)


def pass_y(x, step):
    return lax.ppermute(x, "pcol", [(at, at ^ step) for at in range(NC)])


def pass_prow(x, step):
    return lax.ppermute(x, "prow", [(at, at ^ step) for at in range(NP)])


def by_place(parts, index, count):
    parts = jnp.stack(parts)
    return jnp.stack(
        [lax.dynamic_index_in_dim(parts, index ^ place, 0, False) for place in range(count)]
    )


def swap_z(x):
    return lax.all_to_all(x, "pcol", 0, 0, axis_index_groups=Z_GROUPS, tiled=True)


def swap_pcol(x):
    return lax.all_to_all(x, "pcol", 0, 0, tiled=True)


def swap_prow(x):
    return lax.all_to_all(x, "prow", 0, 0, tiled=True)


def to_all(x, count):
    return jnp.broadcast_to(x[None], (count,) + x.shape)


def total(x):
    return jnp.sum(x.astype(F32), axis=0)


def choose(values, index):
    where = (index[:, None] == jnp.arange(values.shape[0])[None, :]).astype(BF)
    flat = jnp.dot(where, values.reshape(values.shape[0], -1), preferred_element_type=F32)
    return flat.astype(BF).reshape((index.shape[0],) + values.shape[1:])


def dot_nt(a, b):
    return lax.dot_general(a, b, (((1,), (1,)), ((), ())), preferred_element_type=F32)


def dot_nn(a, b):
    return jnp.dot(a, b, preferred_element_type=F32)


def place_mask(place):
    return lax.broadcasted_iota(jnp.int32, (ROWS, TILE), 0) % PER == place


def lower_part(resid, inverse):
    full = dot_nt(resid, inverse[...].reshape(NB, TILE))
    part = full[:, :TILE]
    for place in range(1, PER):
        part = jnp.where(place_mask(place), full[:, place * TILE : (place + 1) * TILE], part)
    return part.astype(BF)


def call(kernel, name, outs, in_specs, args, scratch=(), out_specs=None, grant=None):
    return pl.pallas_call(
        kernel,
        out_shape=tuple(jax.ShapeDtypeStruct(shape, dtype) for shape, dtype in outs),
        in_specs=in_specs,
        out_specs=tuple(out_specs or [VMEM] * len(outs)),
        scratch_shapes=list(scratch),
        compiler_params=pltpu.CompilerParams(vmem_limit_bytes=grant or 8 << 20),
        name=name,
    )(*args)


def pos_kernel(tile_of, pos):
    stride = tile_of.shape[0] // NC

    def put(index, carry):
        pos[tile_of[index * stride]] = index
        return carry

    lax.fori_loop(0, NC, put, 0)


def plane():
    col = lax.axis_index("pcol")
    return col // NY, col % NY


def plane_tile(tile_of, z, other):
    return tile_of[(z * NY + other) * (tile_of.shape[0] // NC)]


def first_kernel(tile_of, got, inverses, tiles, message):
    z, y = plane()
    for index in range(NZ):
        message[index, pl.ds(0, ROWS), :] = jnp.zeros((ROWS, TILE), BF)
        message[index, pl.ds(ROWS, (STEPS - 1) * PIECE), :] = inverses[...]
    for step in range(NY):
        other = y ^ step
        value = got[other, pl.ds(0, ROWS), :].astype(F32)
        value = value + got[other, pl.ds(ROWS, ROWS), :].astype(F32)
        tiles[step] = value
        tile = plane_tile(tile_of, z, other)

        @pl.when(tile // PER == 0)
        def _():
            message[tile % PER, pl.ds(0, ROWS), :] = value.astype(BF)


def stacked_rows(got, at):
    return jnp.concatenate([got[other, pl.ds(at, PIECE), :] for other in range(NY)], axis=0)


def inverse_kernel(tile_of, back, got, message, picked):
    mine = jnp.sum(back[:, pl.ds(0, ROWS), :].astype(F32), axis=0).astype(BF)
    part = dot_nn(mine, stacked_rows(got, UPPER_FIRST)).astype(BF)
    for index in range(NZ):
        message[index] = part
    z, _ = plane()
    for other in range(NY):
        tile = plane_tile(tile_of, z, other)
        near = back[tile % PER, pl.ds(ROWS, PIECE), :]
        far = back[tile % PER, pl.ds(ROWS + PIECE, PIECE), :]
        one = (tile // PER == 1).astype(BF)
        two = (tile // PER == 2).astype(BF)
        picked[other] = near * one + far * two


def update_kernel(step, back, own, near_1, near_2, near_3, solved_out, message, *outer):
    sums = jnp.sum(back[...].astype(F32), axis=0)
    value = sums[:ROWS].astype(BF)
    solved_out[...] = value
    if outer:
        outer[0][...] = sums[ROWS:]
    for index, near in enumerate((own, near_1, near_2, near_3)):
        update = dot_nn(value, near[pl.ds(step * TILE, TILE), :]).astype(BF)
        for other in range(NP):
            message[other, pl.ds(index * ROWS, ROWS), :] = update


def state_kernel(step, tile_of, back, tiles, parts, *rest):
    z, y = plane()
    sums = jnp.sum(back[...].astype(F32), axis=0)
    message = rest[-1]
    part = jnp.zeros((ROWS, TILE), F32)
    for index in range(NY):
        other = y ^ index
        tile = plane_tile(tile_of, z, other)
        keep = (tile // PER > step).astype(F32)
        value = tiles[index] - keep * sums[index * ROWS : (index + 1) * ROWS]
        if step == 0:
            rest[2][index] = value
        block = (value * (tile // PER == step + 1).astype(F32)).astype(BF)
        weights = jnp.concatenate([parts[sub ^ y, other] for sub in range(NY)], axis=0)
        part = part + dot_nn(block, weights)
    part = part.astype(BF)
    for index in range(NZ):
        message[index, pl.ds(0, ROWS), :] = part
        if step == 0:
            message[index, pl.ds(ROWS, ROWS), :] = rest[0][...]
            message[index, pl.ds(2 * ROWS, ROWS), :] = rest[1][index]


def last_kernel(back, outer, got, solved_out, message):
    value = jnp.sum(back[...].astype(F32), axis=0).astype(BF)
    solved_out[...] = value
    resid = (value.astype(F32) - outer[...]).astype(BF)
    part = dot_nt(resid, stacked_rows(got, LOWER_LAST)).astype(BF)
    for index in range(NP):
        message[index] = part


def share_kernel(back, message):
    value = jnp.sum(back[...].astype(F32), axis=0).astype(BF)
    for index in range(NZ):
        message[index] = value


def fetch_kernel(step, pos, pack, tiles, inverse, sems):
    copies = [
        pltpu.make_async_copy(
            pack.at[pos[(step + 1 + at) * PER + place], pl.ds(LOWER_AT + step * TILE, TILE), :],
            tiles.at[at, :, pl.ds(place * TILE, TILE)],
            sems.at[at * PER + place],
        )
        for at in range(STEPS - 1 - step)
        for place in range(PER)
    ]
    copies.append(
        pltpu.make_async_copy(
            pack.at[:, pl.ds(step * PIECE, PIECE), :], inverse, sems.at[len(copies)]
        )
    )
    for copy in copies:
        copy.start()
    for copy in copies:
        copy.wait()


def fetch_call(step, pos, pack):
    later = STEPS - 1 - step
    return call(
        lambda *refs: fetch_kernel(step, *refs),
        f"fetch_block_{step}",
        [((later, TILE, NB), BF), ((NC, PIECE, TILE), BF)],
        [SMEM, HBM],
        (pos, pack),
        [pltpu.SemaphoreType.DMA((later * PER + 1,))],
        grant=GRANT,
    )


def lower_kernel(step, back, base, tiles, inverse, *rest):
    outs = 2 if step == STEPS - 2 else 3
    known = rest[:-outs]
    value_out, message_out = rest[-outs : len(rest) - outs + 2]
    if step == STEPS - 2:
        pick_own = known[0][...]
        value = jnp.zeros((ROWS, TILE), F32)
        for place in range(PER):
            value = jnp.where(place_mask(place), dot_nn(pick_own, back[place]), value)
        value = value.astype(BF)
    else:
        value = jnp.sum(back[:, pl.ds(0, ROWS), :].astype(F32), axis=0).astype(BF)
        bulk = jnp.sum(back[:, pl.ds(ROWS, back.shape[1] - ROWS), :].astype(F32), axis=0)
        rest[-1][...] = bulk.astype(BF)
    value_out[...] = value
    sums = jnp.zeros((ROWS, TILE), F32)
    for at in range(STEPS - 1 - step):
        solved = value if at == 0 else known[at - 1][...]
        wide = jnp.concatenate(
            [jnp.where(place_mask(place), solved, jnp.zeros_like(solved)) for place in range(PER)],
            axis=1,
        )
        sums = sums + dot_nt(wide, tiles[at])
    sums = jnp.sum(sums.reshape(ROWS // PER, PER, TILE), axis=1, keepdims=True)
    sums = jnp.broadcast_to(sums, (ROWS // PER, PER, TILE)).reshape(ROWS, TILE)
    part = lower_part((base[...] - sums).astype(BF), inverse)
    for index in range(NP):
        message_out[index, pl.ds(0, ROWS), :] = part
        if step == STEPS - 2:
            message_out[index, pl.ds(ROWS, known[1].shape[1]), :] = known[1][index]


def lower_call(step, back, base, weights, known):
    outs = [((ROWS, TILE), BF), ((NP, ROWS, TILE), BF)]
    if step == STEPS - 2:
        outs[1] = ((NP, ROWS + known[1].shape[1], TILE), BF)
    else:
        outs.append(((back.shape[1] - ROWS, TILE), BF))
    return call(
        lambda *refs: lower_kernel(step, *refs),
        f"lower_block_{step}",
        outs,
        [VMEM] * (4 + len(known)),
        (back, base, *weights, *known),
        grant=16 << 20,
    )


def body(rhs, pivots, tile_of, upper_rows, upper_inv, lower_rows, lower_inv, solved):
    col = lax.axis_index("pcol")
    row = lax.axis_index("prow")
    z = col // NY
    y = col % NY
    count, width = rhs.shape
    slots = width // TILE
    rows_z = count // NY
    rows_own = count // NC
    first_tiles = tile_of.reshape(NC, slots)[:, 0]
    my_tile = first_tiles[col]
    my_block = my_tile // PER
    my_place = my_tile % PER

    lower_turned = jnp.swapaxes(lower_inv, 1, 2)
    pack = jnp.concatenate(
        [
            lower_turned[: STEPS - 1].reshape(LOWER_AT, TILE),
            lower_rows[: STEPS - 1, :, :TILE].reshape(PACK - LOWER_AT, TILE),
        ],
        axis=0,
    )
    pack_all = lax.all_gather(pack, "pcol", axis=0)

    local_pivots = pivots - col * width
    own = jnp.take(rhs[:, :TILE], local_pivots[:TILE], axis=1)
    own = own.reshape(NZ, NY, rows_own, TILE).transpose(1, 0, 2, 3).reshape(NY, rows_z, TILE)
    own_high = own.astype(BF)
    own_low = (own - own_high.astype(F32)).astype(BF)
    both = jnp.concatenate([upper_inv[0], lower_turned[STEPS - 1]], axis=0)
    start = swap_y(jnp.concatenate([own_high, own_low, to_all(both, NY)], axis=1))
    tiles, message = call(
        first_kernel,
        "first_state",
        [((NY, ROWS, TILE), F32), ((NZ, ROWS + (STEPS - 1) * PIECE, TILE), BF)],
        [SMEM, VMEM, VMEM],
        (tile_of, start, upper_inv[1:].reshape((STEPS - 1) * PIECE, TILE)),
    )
    upper_pack = upper_rows[: STEPS - 1, :, :TILE].reshape((STEPS - 1) * TILE, TILE)
    near = [upper_pack] + [pass_y(upper_pack, step) for step in range(1, NY)]
    message, solved_now, tile_now = lax.optimization_barrier((message, solved, tile_of))
    (pos,) = call(
        pos_kernel, "tile_places", [((NC,), jnp.int32)], [SMEM], (tile_now,), out_specs=[SMEM]
    )
    message, picked = call(
        inverse_kernel,
        "inverse_part_0",
        [((NZ, ROWS, TILE), BF), ((NY, PIECE, TILE), BF)],
        [SMEM, VMEM, VMEM],
        (tile_of, swap_z(message), start),
    )
    parts = jnp.stack([picked] + [pass_y(picked, step) for step in range(1, NY)])

    slot_known = jnp.where(my_block >= STEPS, solved_now[:, :TILE], 0.0)
    known = jnp.concatenate([slot_known, solved_now[:, TILE:]], axis=1).astype(BF)
    outer = lax.dot_general(
        known, lower_rows, (((1,), (2,)), ((), ())), preferred_element_type=F32
    )
    outer = outer.astype(BF).reshape(NZ, NY, rows_own, STEPS, TILE)
    outer = outer.transpose(1, 0, 2, 3, 4).reshape(NY, NZ * rows_own * STEPS, TILE)
    outer_sum = lax.dynamic_index_in_dim(outer, y, 0, False).astype(F32)
    for other in range(1, NY):
        theirs = lax.dynamic_index_in_dim(outer, y ^ other, 0, False)
        outer_sum = outer_sum + pass_y(theirs, other).astype(F32)
    outer = outer_sum.astype(BF).reshape(NZ, rows_own, STEPS, TILE)
    outer_last = outer[:, :, STEPS - 1].reshape(ROWS, TILE)
    outer_rest = outer[:, :, : STEPS - 1].reshape(NZ, rows_own * (STEPS - 1), TILE)
    outer_rest = jnp.pad(outer_rest, ((0, 0), (0, ROWS - rows_own * (STEPS - 1)), (0, 0)))

    finished = []
    for step in range(STEPS - 1):
        outs = [((ROWS, TILE), BF), ((NP, NY * ROWS, TILE), BF)]
        if step == 1:
            outs.append(((2 * ROWS, TILE), F32))
        value, message, *sums = call(
            lambda *refs: update_kernel(step, *refs),
            f"upper_update_{step}",
            outs,
            [VMEM] * (1 + NY),
            (swap_z(message), *near),
        )
        finished.append(value)
        back = swap_prow(message)
        if step == 0:
            tiles, message = call(
                lambda *refs: state_kernel(0, *refs),
                "next_state_0",
                [((NY, ROWS, TILE), F32), ((NZ, 3 * ROWS, TILE), BF)],
                [SMEM] + [VMEM] * 5,
                (tile_of, back, tiles, parts, outer_last, outer_rest),
            )
        else:
            (message,) = call(
                lambda *refs: state_kernel(1, *refs),
                "next_state_1",
                [((NZ, ROWS, TILE), BF)],
                [SMEM] + [VMEM] * 3,
                (tile_of, back, tiles, parts),
            )

    order = jnp.arange(ROWS)
    pick_own = (
        (order[None, :] // rows_own == z) & (order[None, :] % rows_own == order[:, None] // PER)
    ).astype(BF)
    outer = sums[0][ROWS : ROWS + rows_own * (STEPS - 1)].reshape(rows_own, STEPS - 1, TILE)
    outer = jnp.repeat(outer.transpose(1, 0, 2), PER, axis=1)
    last, message = call(
        last_kernel,
        "last_block",
        [((ROWS, TILE), BF), ((NP, ROWS, TILE), BF)],
        [VMEM] * 3,
        (swap_z(message), sums[0][:ROWS], start),
    )
    finished.append(last)
    bases = [
        jnp.dot(pick_own, finished[step], preferred_element_type=F32) - outer[step]
        for step in range(STEPS - 1)
    ]
    stacked = jnp.concatenate(finished, axis=0)
    pair = jnp.stack([stacked, pass_y(stacked, 1)])
    (message,) = call(
        share_kernel, "share_last", [((NZ, ROWS, TILE), BF)], [VMEM], (swap_prow(message),)
    )
    message, pair, pos_now = lax.optimization_barrier((message, pair, pos))
    weights = fetch_call(1, pos_now, pack_all)
    shared = swap_z(message)

    other = pass_y(pair, 2)
    every = [pair[0], pair[1], other[0], other[1]]
    every = by_place(every, y, NY).reshape(NY, STEPS, NZ, rows_own, TILE)
    every = every.transpose(1, 2, 0, 3, 4).reshape(STEPS, count, TILE)
    bulk = jnp.dot(
        jnp.concatenate(list(every), axis=1),
        upper_rows.reshape(STEPS * TILE, width),
        preferred_element_type=F32,
    )
    window_value = jnp.where(
        my_place == row, lax.dynamic_index_in_dim(every, jnp.minimum(my_block, STEPS - 1), 0, False), 0
    ).astype(F32)
    slot_bulk = jnp.where(my_block < STEPS, window_value, bulk[:, :TILE])
    bulk = jnp.concatenate([slot_bulk, bulk[:, TILE:]], axis=1).astype(BF)
    bulk = bulk.reshape(NP, count // NP * slots, TILE)

    last, message = lower_call(1, shared, bases[1], weights, [pick_own, bulk])
    message, pos_now = lax.optimization_barrier((message, pos))
    weights = fetch_call(0, pos_now, pack_all)
    back = swap_prow(message)
    middle, message, bulk = lower_call(0, back, bases[0], weights, [last])
    message, rhs_now = lax.optimization_barrier((message, rhs))
    state0 = jnp.take(rhs_now, local_pivots, axis=1)
    first = total(swap_prow(message)).astype(BF)

    window = jnp.concatenate([first, middle, last], axis=0)
    window = window.reshape(STEPS, rows_own, PER, TILE).transpose(0, 2, 1, 3)
    window = choose(window.reshape(STEPS * PER, rows_own, TILE), first_tiles)
    window, bulk = lax.optimization_barrier((window, bulk))
    window = swap_pcol(window)
    pair = jnp.stack([bulk, pass_prow(bulk, 1)])
    pairs = [pair] + [pass_prow(pair, step) for step in range(2, NP, 2)]
    bulk = by_place([part[side] for part in pairs for side in range(2)], row, NP)
    bulk = bulk.reshape(count, width).astype(F32)
    slot_forward = jnp.where(my_block < STEPS, bulk[:, :TILE], state0[:, :TILE] - bulk[:, :TILE])
    forward = jnp.concatenate([slot_forward, state0[:, TILE:] - bulk[:, TILE:]], axis=1)
    forward, window = lax.optimization_barrier((forward, window))
    window = window.reshape(count, TILE).astype(F32)
    slot_solution = jnp.where(my_block < STEPS, window, solved[:, :TILE])
    backward = jnp.concatenate([slot_solution, solved[:, TILE:]], axis=1)
    return (forward, backward)


def solution(mesh):
    return jax.shard_map(
        body,
        mesh=mesh,
        in_specs=(
            P(None, "pcol"),
            P("pcol"),
            P(),
            P(None, "prow", "pcol"),
            P(None, "pcol", "prow"),
            P(None, "prow", "pcol"),
            P(None, "prow", "pcol"),
            P(None, "pcol"),
        ),
        out_specs=(P(None, "pcol"), P(None, "pcol")),
        check_vma=False,
    )
```
